256 devices in a mesh: dp: 8 (over z_hi, core), tile: 32 (over y, x, z_lo).
Axes of the slice: x: 4, y: 4, z: 8 (z_hi: 4, z_lo: 2; z = z_hi * 2 + z_lo), core: 2. Of those that a mesh axis runs over, the one named last changes fastest.
Arguments:
- tokens: bfloat16 [8, 4096, 1024], P('dp', 'tile'), may hold values from -13 to 13
- timestep: int32 [8], P('dp'), may hold values from 0 to 999
- table: bfloat16 [1000, 2048], replicated, may hold values from -2.5 to 2.5
- w_qkv: bfloat16 [1024, 3072], replicated, may hold values from -0.197858 to 0.197858
- grad_out: bfloat16 [8, 4096, 1024], P('dp', 'tile'), may hold values from -6 to 6
Outputs:
- attended: bfloat16 [8, 4096, 1024], P('dp', 'tile')
- token_gradient: bfloat16 [8, 4096, 1024], P('dp', 'tile')
- modulation_grads: float32 [8, 2048], P('dp')
- grad_wqkv: float32 [1024, 3072], P('tile')
The draws below stay inside these ranges and needn't reach their ends.
All inputs are finite; a program needn't handle non-finite values.
Results may differ from the reference program's by a relative error of at most 0.019.
The reference program's roundings to bfloat16 on the way count: a program that leaves them out, or rounds other values in their place, can miss the bound.
Values may be sent and summed in bfloat16 or wider, within the bound.
No kernel may reach another device: no remote copies, remote signals or barrier semaphores. Data moves between devices by JAX's collectives and lax.ppermute only.
A program may use at most 128 MiB of HBM per device.

```python
import math
import jax
import jax.numpy as jnp
from jax import lax

D = 1024
HEADS = 16
STEPS = 1000
TOKENS = 4096
IMAGES = 8


def draw_tokens(key, part):
    key = jax.random.fold_in(key, 3)
    subkeys = jax.random.split(key, 1)
    sampled = jax.random.truncated_normal(subkeys[0], -6.0, 6.0, (IMAGES, TOKENS, D), jnp.float32)
    return sampled.astype(jnp.bfloat16)


def draw_w_qkv(key, part):
    key = jax.random.fold_in(key, 5)
    subkeys = jax.random.split(key, 1)
    sampled = jax.random.truncated_normal(subkeys[0], -6.0, 6.0, (D, 3 * D), jnp.float32) * (1.0 / math.sqrt(D))
    return sampled.astype(jnp.bfloat16)


def set_ends(result, rng, least, top_value):
    longest = result.shape.index(max(result.shape))
    spots = []
    for shift in (0, 1):
        where = [jax.random.randint(jax.random.fold_in(rng, axis), (), 0, length) for axis, length in enumerate(result.shape)]
        where[longest] = (where[longest] + shift) % result.shape[longest]
        spots.append(tuple(where))
    return result.at[spots[0]].set(least).at[spots[1]].set(top_value)


def shard_levels(own_key, extent, cuts, low, top_value):
    gain, own = 1.0, jax.random.fold_in(own_key, 6)
    for axis_at, blocks in cuts:
        draws = jnp.exp(jax.random.uniform(jax.random.fold_in(own, axis_at), (blocks,), jnp.float32, low / len(cuts), top_value / len(cuts)))
        gain = gain * jnp.repeat(draws, extent[axis_at] // blocks).reshape([-1 if axis == axis_at else 1 for axis in range(len(extent))])
    return gain


def scatter_about(key, shape, scale, reach, cuts=(), kind=jnp.bfloat16):
    factor_of = shard_levels(key, shape, cuts, -0.22, 0.18) if cuts else 1.0
    values = jax.random.normal(key, shape, jnp.float32) * scale * factor_of
    return jnp.minimum(jnp.maximum(values, -reach), reach).astype(kind)


def setup_inputs(seed: int = 0) -> dict:
    splits = jax.random.split(jax.random.key(seed), 6)
    return {
        "tokens": draw_tokens(jax.random.fold_in(splits[5], 71), 0),
        "timestep": set_ends(jax.random.randint(splits[1], (IMAGES,), 0, STEPS), jax.random.fold_in(splits[1], 1), 0, STEPS - 1).astype(jnp.int32),
        "table": scatter_about(splits[2], (STEPS, 2 * D), 0.5, 2.5),
        "w_qkv": draw_w_qkv(jax.random.fold_in(splits[5], 71), 0),
        "grad_out": scatter_about(splits[4], (IMAGES, TOKENS, D), 1.0, 6.0, ((0, 8), (1, 32))),
    }


def head_pass(queries, keys, values, grads):
    rows = queries.shape[0]
    depth = queries.shape[1]
    factor = depth ** (-0.5)
    block = math.gcd(rows, 512)
    count = rows // block
    q_blocks = queries.reshape(count, block, depth)
    g_blocks = grads.reshape(count, block, depth)

    def step(carry, item):
        key_grad, value_grad = carry
        q_part, g_part = item
        scores = lax.dot_general(q_part, keys, (((1,), (1,)), ((), ())), preferred_element_type=jnp.float32) * factor
        top = lax.optimization_barrier(jnp.max(scores, axis=1, keepdims=True))
        expo = jnp.exp(scores - top)
        probs = expo / lax.optimization_barrier(jnp.sum(expo, axis=1, keepdims=True))
        probs_low = probs.astype(jnp.bfloat16)
        output = jnp.dot(probs_low, values, preferred_element_type=jnp.float32)
        dprob = lax.dot_general(g_part, values, (((1,), (1,)), ((), ())), preferred_element_type=jnp.float32)
        delta = lax.optimization_barrier(jnp.sum(g_part.astype(jnp.float32) * output, axis=1, keepdims=True))
        dscore = (probs * (dprob - delta)).astype(jnp.bfloat16)
        query_grad = jnp.dot(dscore, keys, preferred_element_type=jnp.float32) * factor
        key_grad = key_grad + lax.dot_general(dscore, q_part, (((0,), (0,)), ((), ())), preferred_element_type=jnp.float32) * factor
        value_grad = value_grad + lax.dot_general(probs_low, g_part, (((0,), (0,)), ((), ())), preferred_element_type=jnp.float32)
        return ((key_grad, value_grad), (output, query_grad))
    start = (jnp.zeros(keys.shape, jnp.float32), jnp.zeros(values.shape, jnp.float32))
    (key_grad, value_grad), (output, query_grad) = lax.scan(step, start, (q_blocks, g_blocks))
    return (output.reshape(rows, depth), query_grad.reshape(rows, depth), key_grad, value_grad)

def one_image(x_in, step_index, table, w_qkv, g_out):
    width = x_in.shape[1]
    ntok = x_in.shape[0]
    depth = width // HEADS
    onehot = (jnp.arange(table.shape[0], dtype=jnp.int32) == step_index).astype(jnp.bfloat16)
    mod = jnp.dot(onehot[None, :], table, preferred_element_type=jnp.float32)[0]
    scale_factor = mod[:width]
    shift_offset = mod[width:]
    tokens_float = x_in.astype(jnp.float32)
    inverse_deviation = 1.0 / jnp.sqrt(lax.optimization_barrier(jnp.mean(tokens_float * tokens_float, axis=1, keepdims=True)) + 1e-06)
    centered_scaled = tokens_float * inverse_deviation
    normalized_tokens = (centered_scaled * (1.0 + scale_factor) + shift_offset).astype(jnp.bfloat16)
    qkv = jnp.dot(normalized_tokens, w_qkv, preferred_element_type=jnp.float32).astype(jnp.bfloat16)

    def split(block):
        return block.reshape(ntok, HEADS, depth).transpose(1, 0, 2)
    heads_q = split(qkv[:, :width])
    heads_k = split(qkv[:, width:2 * width])
    heads_v = split(qkv[:, 2 * width:])
    heads_g = split(g_out)
    output, query_grad, key_grad, value_grad = lax.map(lambda a: head_pass(*a), (heads_q, heads_k, heads_v, heads_g))

    def join(block):
        return block.transpose(1, 0, 2).reshape(ntok, width)
    attended = join(output).astype(jnp.bfloat16)
    dqkv = jnp.concatenate([join(query_grad), join(key_grad), join(value_grad)], axis=1).astype(jnp.bfloat16)
    normalized_grad = lax.dot_general(dqkv, w_qkv, (((1,), (1,)), ((), ())), preferred_element_type=jnp.float32)
    weight_grad = lax.dot_general(normalized_tokens, dqkv, (((0,), (0,)), ((), ())), preferred_element_type=jnp.float32)
    modulation_grads = jnp.concatenate([lax.optimization_barrier(jnp.sum(normalized_grad * centered_scaled, axis=0)), lax.optimization_barrier(jnp.sum(normalized_grad, axis=0))])
    norm_input_grad = normalized_grad * (1.0 + scale_factor)
    token_gradient = (inverse_deviation * (norm_input_grad - centered_scaled * lax.optimization_barrier(jnp.mean(norm_input_grad * centered_scaled, axis=1, keepdims=True)))).astype(jnp.bfloat16)
    return (attended, token_gradient, modulation_grads, weight_grad)

def reference(tokens, timestep, table, w_qkv, grad_out):
    attended, token_gradient, modulation_grads, weight_grads = lax.map(lambda a: one_image(a[0], a[1], table, w_qkv, a[2]), (tokens, timestep, grad_out))
    return (attended, token_gradient, modulation_grads, lax.optimization_barrier(jnp.sum(weight_grads, axis=0)))
```

```python
import functools

import jax
import jax.numpy as jnp
from jax import lax
from jax.experimental import pallas as pl
from jax.experimental.pallas import tpu as pltpu
from jax.sharding import PartitionSpec as P

HEADS = 16
DEPTH = 64
LOG2E = 1.4426950408889634
BF16 = jnp.bfloat16
F32 = jnp.float32
EVERY = ("dp", "tile")

SWAP = [
    ((zh * 2 + core) * 32 + yx * 2 + zl, (zh * 2 + zl) * 32 + yx * 2 + core)
    for zh in range(4)
    for core in range(2)
    for yx in range(16)
    for zl in range(2)
]
PLANE = [[yx * 2 + zl for yx in range(16)] for zl in range(2)]
OTHER_CORE = [(d, d ^ 1) for d in range(8)]


def swap(x):
    return lax.ppermute(x, EVERY, SWAP)


def plane_exchange(x):
    return lax.all_to_all(
        x, "tile", split_axis=0, concat_axis=0, tiled=True, axis_index_groups=PLANE
    )


def dot(a, b):
    return jnp.dot(a, b, preferred_element_type=F32)


def dot_t(a, b):
    return lax.dot_general(a, b, (((1,), (1,)), ((), ())), preferred_element_type=F32)


def low_lanes(shape):
    return lax.broadcasted_iota(jnp.int32, shape, 1) < DEPTH


def project_kernel(x_ref, g_ref, mod_ref, wq_ref, wk_ref, wv_ref, normed_ref, out_ref):
    @pl.when(pl.program_id(0) == 0)
    def _():
        x = x_ref[...].astype(F32)
        inv = 1.0 / jnp.sqrt(jnp.mean(x * x, axis=1, keepdims=True) + 1e-06)
        mod = mod_ref[...].astype(F32)
        normed_ref[...] = ((x * inv) * (1.0 + mod[0:1]) + mod[1:2]).astype(BF16)

    normed = normed_ref[...]
    q = dot(normed, wq_ref[...]).astype(BF16).astype(F32)
    k = dot(normed, wk_ref[...]).astype(BF16).astype(F32)
    v = dot(normed, wv_ref[...]).astype(BF16).astype(F32)
    g = g_ref[...].astype(F32)
    low = low_lanes(q.shape)
    out_ref[0, 0:128] = jnp.where(low, q, pltpu.roll(g, DEPTH, 1)).astype(BF16)
    out_ref[0, 128:256] = jnp.where(low, k, pltpu.roll(v, DEPTH, 1)).astype(BF16)
    out_ref[1, 0:128] = jnp.where(low, pltpu.roll(q, DEPTH, 1), g).astype(BF16)
    out_ref[1, 128:256] = jnp.where(low, pltpu.roll(k, DEPTH, 1), v).astype(BF16)


def project(x, g, mod, w):
    return pl.pallas_call(
        project_kernel,
        grid=(HEADS // 2,),
        in_specs=[
            pl.BlockSpec((128, 1024), lambda i: (0, 0)),
            pl.BlockSpec((128, 128), lambda i: (0, i)),
            pl.BlockSpec((2, 1024), lambda i: (0, 0)),
            pl.BlockSpec((1024, 128), lambda i: (0, i)),
            pl.BlockSpec((1024, 128), lambda i: (0, 8 + i)),
            pl.BlockSpec((1024, 128), lambda i: (0, 16 + i)),
        ],
        out_specs=[
            pl.BlockSpec((128, 1024), lambda i: (0, 0)),
            pl.BlockSpec((2, 256, 128), lambda i: (i, 0, 0)),
        ],
        out_shape=[
            jax.ShapeDtypeStruct((128, 1024), BF16),
            jax.ShapeDtypeStruct((HEADS, 256, 128), BF16),
        ],
        compiler_params=pltpu.CompilerParams(dimension_semantics=("arbitrary",)),
        cost_estimate=pl.CostEstimate(
            flops=2 * 128 * 1024 * 3072, bytes_accessed=8 << 20, transcendentals=0
        ),
        name="project",
    )(x, g, mod, w, w, w)


def attention_kernel(
    bq, kt, recv_ref, kvp_ref, dqo_ref, own_ref, other_ref, kv, kvt, acc, s_scr, dp_scr, pb_scr
):
    i = pl.program_id(0)
    nk = kv.shape[0]
    half = nk // 2
    tiles = [pl.ds(t * kt, kt) for t in range(nk // kt)]

    @pl.when(i == 0)
    def _():
        kv[:half] = recv_ref[:, 128:, :].reshape(half, 128)
        kv[half:] = kvp_ref[...].reshape(half, 128)
        acc[...] = jnp.zeros_like(acc)
        for t in tiles:
            kvt[:, t] = kv[t].T

    srcs = bq // 128
    qg = recv_ref[pl.ds(i * srcs, srcs), :128, :].reshape(bq, 128)
    low = low_lanes(qg.shape)
    zero = jnp.zeros_like(qg)
    q0 = jnp.where(low, qg * jnp.asarray(0.125, BF16), zero)
    g0 = jnp.where(low, zero, qg)
    q0t = q0.T
    g0t = g0.T
    top = jnp.full((8, bq), -jnp.inf, F32)
    for t in tiles:
        s = dot(kv[t], q0t)
        s_scr[t] = s
        top = jnp.maximum(top, jnp.max(s.reshape(kt // 8, 8, bq), axis=0))
    top = jnp.max(top, axis=0, keepdims=True)
    total = jnp.zeros((8, bq), F32)
    for t in tiles:
        e = jnp.exp2((s_scr[t] - top) * LOG2E)
        s_scr[t] = e
        total = total + jnp.sum(e.reshape(kt // 8, 8, bq), axis=0)
        dp_scr[t] = dot(kv[t], g0t)
    inv = 1.0 / jnp.sum(total, axis=0, keepdims=True)
    o_t = jnp.zeros((DEPTH, bq), F32)
    for t in tiles:
        pb = (s_scr[t] * inv).astype(BF16)
        pb_scr[t] = pb
        o_t = o_t + dot(kvt[DEPTH:, t], pb)
    delta = jnp.sum(o_t * g0t[DEPTH:].astype(F32), axis=0, keepdims=True)
    dq_t = jnp.zeros((DEPTH, bq), F32)
    for t in tiles:
        ds = ((s_scr[t] * inv) * (dp_scr[t] - delta)).astype(BF16)
        dq_t = dq_t + dot(kvt[:DEPTH, t], ds)
        acc[t] += dot(ds, q0) + dot(pb_scr[t], g0)
    dqo = jnp.concatenate([dq_t * 0.125, o_t], axis=0).T.astype(BF16)
    dqo_ref[...] = dqo.reshape(srcs, 128, 128)

    @pl.when(i == pl.num_programs(0) - 1)
    def _():
        own_ref[...] = acc[:half].reshape(16, 128, 128)
        other_ref[...] = acc[half:].astype(BF16).reshape(16, 128, 128)


def attention(recv, kvp, bq=512, kt=256):
    nq, nk = 2048, 4096
    srcs = bq // 128
    whole = lambda i: (0, 0, 0)
    return pl.pallas_call(
        functools.partial(attention_kernel, bq, kt),
        grid=(nq // bq,),
        in_specs=[
            pl.BlockSpec((16, 256, 128), whole),
            pl.BlockSpec((16, 128, 128), whole),
        ],
        out_specs=[
            pl.BlockSpec((srcs, 128, 128), lambda i: (i, 0, 0)),
            pl.BlockSpec((16, 128, 128), whole),
            pl.BlockSpec((16, 128, 128), whole),
        ],
        out_shape=[
            jax.ShapeDtypeStruct((16, 128, 128), BF16),
            jax.ShapeDtypeStruct((16, 128, 128), F32),
            jax.ShapeDtypeStruct((16, 128, 128), BF16),
        ],
        scratch_shapes=[
            pltpu.VMEM((nk, 128), BF16),
            pltpu.VMEM((128, nk), BF16),
            pltpu.VMEM((nk, 128), F32),
            pltpu.VMEM((nk, bq), F32),
            pltpu.VMEM((nk, bq), F32),
            pltpu.VMEM((nk, bq), BF16),
        ],
        compiler_params=pltpu.CompilerParams(
            vmem_limit_bytes=56 * 1024 * 1024, dimension_semantics=("arbitrary",)
        ),
        cost_estimate=pl.CostEstimate(
            flops=6 * 2 * nq * nk * 256, bytes_accessed=4 << 20, transcendentals=nq * nk
        ),
        name="attention",
    )(recv, kvp)


def weight_kernel(normed_ref, back_ref, out_ref, back_t):
    @pl.when(pl.program_id(0) == 0)
    def _():
        for s in range(16):
            back_t[:128, s * 128 : (s + 1) * 128] = back_ref[s, :128].T
            back_t[128:, s * 128 : (s + 1) * 128] = back_ref[s, 128:].T

    out_ref[...] = dot(back_t[...], normed_ref[...]).T.astype(BF16)


def weight_grad(normed, back):
    return pl.pallas_call(
        weight_kernel,
        grid=(4,),
        in_specs=[
            pl.BlockSpec((2048, 256), lambda i: (0, i)),
            pl.BlockSpec((16, 256, 128), lambda i: (0, 0, 0)),
        ],
        out_specs=pl.BlockSpec((256, 256), lambda i: (i, 0)),
        out_shape=jax.ShapeDtypeStruct((1024, 256), BF16),
        scratch_shapes=[pltpu.VMEM((256, 2048), BF16)],
        compiler_params=pltpu.CompilerParams(
            vmem_limit_bytes=32 * 1024 * 1024, dimension_semantics=("arbitrary",)
        ),
        cost_estimate=pl.CostEstimate(
            flops=2 * 2048 * 1024 * 256, bytes_accessed=6 << 20, transcendentals=0
        ),
        name="weight_grad",
    )(normed, back)


def token_kernel(
    x_ref, mod_ref, back_ref, wq_ref, wk_ref, wv_ref, att_ref, grad_ref, sums_ref, acc
):
    i = pl.program_id(0)
    low = low_lanes((128, 128))
    a = back_ref[0].astype(F32)
    b = back_ref[1].astype(F32)
    a_roll = pltpu.roll(a, DEPTH, 1)
    b_roll = pltpu.roll(b, DEPTH, 1)
    dq = jnp.where(low, a[:128], b_roll[:128]).astype(BF16)
    att_ref[...] = jnp.where(low, a_roll[:128], b[:128]).astype(BF16)
    dk = jnp.where(low, a[128:], b_roll[128:]).astype(BF16)
    dv = jnp.where(low, a_roll[128:], b[128:]).astype(BF16)
    part = dot_t(dq, wq_ref[...]) + dot_t(dk, wk_ref[...]) + dot_t(dv, wv_ref[...])

    @pl.when(i == 0)
    def _():
        acc[...] = part

    @pl.when(i > 0)
    def _():
        acc[...] += part

    @pl.when(i == pl.num_programs(0) - 1)
    def _():
        x = x_ref[...].astype(F32)
        inv = 1.0 / jnp.sqrt(jnp.mean(x * x, axis=1, keepdims=True) + 1e-06)
        xhat = x * inv
        dn = acc[...]
        sums_ref[0:1] = jnp.sum(dn * xhat, axis=0, keepdims=True)
        sums_ref[1:2] = jnp.sum(dn, axis=0, keepdims=True)
        gn = dn * (1.0 + mod_ref[0:1].astype(F32))
        grad_ref[...] = (
            inv * (gn - xhat * jnp.mean(gn * xhat, axis=1, keepdims=True))
        ).astype(BF16)


def token_grad(x, mod, back, w):
    return pl.pallas_call(
        token_kernel,
        grid=(HEADS // 2,),
        in_specs=[
            pl.BlockSpec((128, 1024), lambda i: (0, 0)),
            pl.BlockSpec((2, 1024), lambda i: (0, 0)),
            pl.BlockSpec((2, 256, 128), lambda i: (i, 0, 0)),
            pl.BlockSpec((1024, 128), lambda i: (0, i)),
            pl.BlockSpec((1024, 128), lambda i: (0, 8 + i)),
            pl.BlockSpec((1024, 128), lambda i: (0, 16 + i)),
        ],
        out_specs=[
            pl.BlockSpec((128, 128), lambda i: (0, i)),
            pl.BlockSpec((128, 1024), lambda i: (0, 0)),
            pl.BlockSpec((2, 1024), lambda i: (0, 0)),
        ],
        out_shape=[
            jax.ShapeDtypeStruct((128, 1024), BF16),
            jax.ShapeDtypeStruct((128, 1024), BF16),
            jax.ShapeDtypeStruct((2, 1024), F32),
        ],
        scratch_shapes=[pltpu.VMEM((128, 1024), F32)],
        compiler_params=pltpu.CompilerParams(dimension_semantics=("arbitrary",)),
        cost_estimate=pl.CostEstimate(
            flops=2 * 128 * 1024 * 3072, bytes_accessed=8 << 20, transcendentals=0
        ),
        name="token_grad",
    )(x, mod, back, w, w, w)


def on_device(tokens, timestep, table, w_qkv, grad_out):
    row = lax.dynamic_slice(table, (timestep[0], 0), (1, table.shape[1])).reshape(2, 1024)
    x = swap(tokens[0])
    mod = swap(row)
    g = swap(grad_out[0])
    normed, sent = project(x, g, mod, w_qkv)
    recv = plane_exchange(sent)
    normed_all = lax.all_gather(normed, "tile", axis_index_groups=PLANE, tiled=True)
    kvp = lax.ppermute(recv[:, 128:], "dp", OTHER_CORE)
    dqo, own, other = attention(recv, kvp)
    mine = lax.ppermute(other, "dp", OTHER_CORE)
    dkv = (own + mine.astype(F32)).astype(BF16)
    back = jnp.concatenate([dqo, dkv], axis=1)
    back_recv = plane_exchange(back)
    partial = weight_grad(normed_all, back)
    pieces = lax.all_to_all(
        partial.reshape(256, 4, 256), ("tile", "dp"), split_axis=0, concat_axis=0, tiled=True
    )
    attended, token_gradient, sums = token_grad(x, mod, back_recv, w_qkv)
    attended = swap(attended)
    token_gradient = swap(token_gradient)
    sums = sums + lax.ppermute(sums, "dp", OTHER_CORE)
    for bit in (2, 4, 8, 16):
        sums = sums + lax.ppermute(sums, "tile", [(t, t ^ bit) for t in range(32)])
    sums = swap(sums)
    rows = jnp.sum(pieces.astype(F32).reshape(16, 16, 4, 256), axis=1)
    rows = jnp.stack([rows[:, :, :64], rows[:, :, 128:192], rows[:, :, 192:]], axis=0)
    rows = rows.transpose(2, 0, 1, 3).reshape(4, 3072).astype(BF16)
    grad_wqkv = lax.all_gather(rows, "dp", tiled=True).astype(F32)
    return (
        attended[None],
        token_gradient[None],
        sums.reshape(1, 2048),
        grad_wqkv,
    )


def solution(mesh):
    placed = (P("dp", "tile", None), P("dp"), P(), P(), P("dp", "tile", None))
    return jax.shard_map(
        on_device,
        mesh=mesh,
        in_specs=placed,
        out_specs=(P("dp", "tile", None), P("dp", "tile", None), P("dp", None), P("tile", None)),
        check_vma=False,
    )
```

```python
import functools

import jax
import jax.numpy as jnp
from jax import lax
from jax.experimental import pallas as pl
from jax.experimental.pallas import tpu as pltpu
from jax.sharding import PartitionSpec as P

HEADS = 16
DEPTH = 64
WIDTH = 1024
TOK = 128
LOG2E = 1.4426950408889634
BF16 = jnp.bfloat16
F32 = jnp.float32
MIB = 1024 * 1024

SWAP = [
    ((zh * 2 + core) * 32 + yx * 2 + zl, (zh * 2 + zl) * 32 + yx * 2 + core)
    for zh in range(4)
    for core in range(2)
    for yx in range(16)
    for zl in range(2)
]
PLANE = [[yx * 2 + zl for yx in range(16)] for zl in range(2)]
OTHER_CORE = [(d, d ^ 1) for d in range(8)]


def swap(x):
    return lax.ppermute(x, ("dp", "tile"), SWAP)


def from_other_core(x):
    return lax.ppermute(x, "dp", OTHER_CORE)


def plane_exchange(x):
    return lax.all_to_all(
        x, "tile", split_axis=0, concat_axis=0, tiled=True, axis_index_groups=PLANE
    )


def dot(a, b):
    return jnp.dot(a, b, preferred_element_type=F32)


def dot_t(a, b):
    return lax.dot_general(a, b, (((1,), (1,)), ((), ())), preferred_element_type=F32)


def low_lanes(shape):
    return lax.broadcasted_iota(jnp.int32, shape, len(shape) - 1) < DEPTH


def pairs(low, a, b):
    axis = a.ndim - 1
    return jnp.where(low, a, pltpu.roll(b, DEPTH, axis)), jnp.where(
        low, pltpu.roll(a, DEPTH, axis), b
    )


def project_kernel(x_ref, g_ref, mod_ref, wq_ref, wk_ref, wv_ref, copies_ref, out_ref, normed_ref, xhat_ref):
    @pl.when(pl.program_id(0) == 0)
    def _():
        x = x_ref[...].astype(F32)
        inv = 1.0 / jnp.sqrt(jnp.mean(x * x, axis=1, keepdims=True) + 1e-06)
        mod = mod_ref[...].astype(F32)
        xhat = x * inv
        xhat_ref[...] = xhat.astype(BF16)
        normed_ref[...] = (xhat * (1.0 + mod[0:1]) + mod[1:2]).astype(BF16)

    normed = normed_ref[...]
    for c in range(copies_ref.shape[0]):
        copies_ref[c] = xhat_ref[...]
    q4 = dot(normed, wq_ref[...]).astype(BF16).astype(F32)
    k4 = dot(normed, wk_ref[...]).astype(BF16).astype(F32)
    v4 = dot(normed, wv_ref[...]).astype(BF16).astype(F32)
    g4 = g_ref[...].astype(F32)
    low = low_lanes((TOK, 128))
    for p in range(2):
        lanes = slice(p * 128, (p + 1) * 128)
        for rows, a, b in ((slice(0, TOK), q4, g4), (slice(TOK, 2 * TOK), k4, v4)):
            first, second = pairs(low, a[:, lanes], b[:, lanes])
            out_ref[2 * p, rows] = first.astype(BF16)
            out_ref[2 * p + 1, rows] = second.astype(BF16)


def weight_specs():
    return [pl.BlockSpec((WIDTH, 256), lambda i, c=c: (0, 4 * c + i)) for c in range(3)]


def project(packed, w):
    return pl.pallas_call(
        project_kernel,
        grid=(4,),
        in_specs=[
            pl.BlockSpec((TOK, WIDTH), lambda i: (0, 0)),
            pl.BlockSpec((TOK, 256), lambda i: (1, i)),
            pl.BlockSpec((16, WIDTH), lambda i: (16, 0)),
        ]
        + weight_specs(),
        out_specs=[
            pl.BlockSpec((4, TOK, WIDTH), lambda i: (i, 0, 0)),
            pl.BlockSpec((4, 2 * TOK, 128), lambda i: (i, 0, 0)),
        ],
        out_shape=[
            jax.ShapeDtypeStruct((HEADS, TOK, WIDTH), BF16),
            jax.ShapeDtypeStruct((HEADS, 2 * TOK, 128), BF16),
        ],
        scratch_shapes=[pltpu.VMEM((TOK, WIDTH), BF16)] * 2,
        compiler_params=pltpu.CompilerParams(
            vmem_limit_bytes=60 * MIB, dimension_semantics=("arbitrary",)
        ),
        cost_estimate=pl.CostEstimate(
            flops=2 * TOK * WIDTH * 3 * WIDTH, bytes_accessed=12 * MIB, transcendentals=0
        ),
        name="project",
    )(packed, packed, packed, w, w, w)


def attention_kernel(
    bq, kt, recv_ref, kvp_ref, back_ref, own_ref, other_ref, kv, kvt, acc, s_scr, dp_scr, pb_scr
):
    i = pl.program_id(0)
    nk = kv.shape[0]
    half = nk // 2
    tiles = [pl.ds(t * kt, kt) for t in range(nk // kt)]

    @pl.when(i == 0)
    def _():
        kv[:half] = recv_ref[:, 128:, :].reshape(half, 128)
        kv[half:] = kvp_ref[...].reshape(half, 128)
        acc[...] = jnp.zeros_like(acc)
        for t in tiles:
            kvt[:, t] = kv[t].T

    srcs = bq // 128
    qg = recv_ref[pl.ds(i * srcs, srcs), :128, :].reshape(bq, 128)
    low = low_lanes(qg.shape)
    zero = jnp.zeros_like(qg)
    q0 = jnp.where(low, qg * jnp.asarray(0.125, BF16), zero)
    g0 = jnp.where(low, zero, qg)
    q0t = q0.T
    g0t = g0.T
    top = jnp.full((8, bq), -jnp.inf, F32)
    for t in tiles:
        s = dot(kv[t], q0t)
        s_scr[t] = s
        top = jnp.maximum(top, jnp.max(s.reshape(kt // 8, 8, bq), axis=0))
    top = jnp.max(top, axis=0, keepdims=True)
    total = jnp.zeros((8, bq), F32)
    for t in tiles:
        e = jnp.exp2((s_scr[t] - top) * LOG2E)
        s_scr[t] = e
        total = total + jnp.sum(e.reshape(kt // 8, 8, bq), axis=0)
        dp_scr[t] = dot(kv[t], g0t)
    inv = 1.0 / jnp.sum(total, axis=0, keepdims=True)
    o_t = jnp.zeros((DEPTH, bq), F32)
    for t in tiles:
        pb = (s_scr[t] * inv).astype(BF16)
        pb_scr[t] = pb
        o_t = o_t + dot(kvt[DEPTH:, t], pb)
    delta = jnp.sum(o_t * g0t[DEPTH:].astype(F32), axis=0, keepdims=True)
    dq_t = jnp.zeros((DEPTH, bq), F32)
    for t in tiles:
        ds = ((s_scr[t] * inv) * (dp_scr[t] - delta)).astype(BF16)
        dq_t = dq_t + dot(kvt[:DEPTH, t], ds)
        acc[t] += dot(ds, q0) + dot(pb_scr[t], g0)
    dqo = jnp.concatenate([dq_t * 0.125, o_t], axis=0).T.astype(BF16)
    back_ref[:, :128] = dqo.reshape(srcs, 128, 128)

    @pl.when(i == pl.num_programs(0) - 1)
    def _():
        own_ref[...] = acc[:half].reshape(16, 128, 128)
        other_ref[...] = acc[half:].astype(BF16).reshape(16, 128, 128)


def attention(recv, kvp, bq=512, kt=256):
    nq, nk = 2048, 4096
    srcs = bq // 128
    whole = lambda i: (0, 0, 0)
    return pl.pallas_call(
        functools.partial(attention_kernel, bq, kt),
        grid=(nq // bq,),
        in_specs=[
            pl.BlockSpec((16, 256, 128), whole),
            pl.BlockSpec((16, 128, 128), whole),
        ],
        out_specs=[
            pl.BlockSpec((srcs, 256, 128), lambda i: (i, 0, 0)),
            pl.BlockSpec((16, 128, 128), whole),
            pl.BlockSpec((16, 128, 128), whole),
        ],
        out_shape=[
            jax.ShapeDtypeStruct((16, 256, 128), BF16),
            jax.ShapeDtypeStruct((16, 128, 128), F32),
            jax.ShapeDtypeStruct((16, 128, 128), BF16),
        ],
        scratch_shapes=[
            pltpu.VMEM((nk, 128), BF16),
            pltpu.VMEM((128, nk), BF16),
            pltpu.VMEM((nk, 128), F32),
            pltpu.VMEM((nk, bq), F32),
            pltpu.VMEM((nk, bq), F32),
            pltpu.VMEM((nk, bq), BF16),
        ],
        compiler_params=pltpu.CompilerParams(
            vmem_limit_bytes=48 * MIB, dimension_semantics=("arbitrary",)
        ),
        cost_estimate=pl.CostEstimate(
            flops=6 * 2 * nq * nk * 256, bytes_accessed=4 << 20, transcendentals=nq * nk
        ),
        name="attention",
    )(recv, kvp)


def combine_kernel(back_ref, own_ref, mine_ref, out_ref):
    out_ref[...] = (own_ref[...] + mine_ref[...].astype(F32)).astype(BF16)


def combine(back, own, mine):
    half = pl.BlockSpec((16, 128, 128), lambda i: (0, 0, 0))
    return pl.pallas_call(
        combine_kernel,
        grid=(1,),
        in_specs=[pl.BlockSpec(memory_space=pl.ANY), half, half],
        out_specs=pl.BlockSpec((16, 128, 128), lambda i: (0, 1, 0)),
        out_shape=jax.ShapeDtypeStruct((16, 256, 128), BF16),
        input_output_aliases={0: 0},
        compiler_params=pltpu.CompilerParams(vmem_limit_bytes=32 * MIB),
        cost_estimate=pl.CostEstimate(flops=1 << 18, bytes_accessed=2 * MIB, transcendentals=0),
        name="combine",
    )(back, own, mine)


def weight_kernel(
    place_ref, xhat_ref, back_ref, mod_ref, wq_ref, wk_ref, wv_ref, keep_ref, send_ref, sums_ref, back_t
):
    @pl.when(pl.program_id(0) == 0)
    def _():
        for s in range(16):
            tokens = slice(s * TOK, (s + 1) * TOK)
            back_t[:128, tokens] = back_ref[s, :TOK].T
            back_t[128:, tokens] = back_ref[s, TOK:].T

    lhs = back_t[...]
    grad_t = dot(lhs, xhat_ref[...])
    column = jnp.sum(lhs.astype(F32), axis=1, keepdims=True)
    odd = place_ref[1] == 1
    scale_sum = jnp.zeros((1, 256), F32)
    shift_sum = jnp.zeros((1, 256), F32)
    for w_ref, first in ((wq_ref, 0), (wk_ref, 128), (wv_ref, 192)):
        w_t = w_ref[...].astype(F32).T
        w_t = jnp.where(odd, w_t[DEPTH:], w_t[:DEPTH])
        rows = slice(first, first + DEPTH)
        scale_sum = scale_sum + jnp.sum(w_t * grad_t[rows], axis=0, keepdims=True)
        shift_sum = shift_sum + jnp.sum(w_t * column[rows], axis=0, keepdims=True)
    sums_ref[0:1] = scale_sum
    sums_ref[1:2] = shift_sum
    mod = mod_ref[...].astype(F32)
    grad = (grad_t * (1.0 + mod[0:1]) + column * mod[1:2]).T
    low = low_lanes((256, 128))
    dq_dk, dv = pairs(low, grad[:, :128], grad[:, 128:])
    dv = dv.reshape(8, 2, 2, 8, 128)
    low = low_lanes((8, 2, 8, 128))
    dv = jnp.where(low, pltpu.roll(dv[:, :, 0], DEPTH, 3), dv[:, :, 1])
    dq_dk = dq_dk.reshape(8, 2, 16, 128)

    def put(ref, half):
        ref[:, :16] = dq_dk[:, half]
        ref[:, 16:] = dv[:, half]

    @pl.when(place_ref[0] == 0)
    def _():
        put(keep_ref, 0)
        put(send_ref, 1)

    @pl.when(place_ref[0] == 1)
    def _():
        put(keep_ref, 1)
        put(send_ref, 0)


def weight_grad(place, xhat, back, packed, w):
    rows = pl.BlockSpec((8, 24, 128), lambda i, place: (i, 0, 0))
    return pl.pallas_call(
        weight_kernel,
        grid_spec=pltpu.PrefetchScalarGridSpec(
            num_scalar_prefetch=1,
            grid=(4,),
            in_specs=[
                pl.BlockSpec((2048, 256), lambda i, place: (0, i)),
                pl.BlockSpec((16, 256, 128), lambda i, place: (0, 0, 0)),
                pl.BlockSpec((16, 256), lambda i, place: (16, i)),
            ]
            + [pl.BlockSpec((256, 128), lambda i, place, c=c: (i, 8 * c + place[2])) for c in range(3)],
            out_specs=[rows, rows, pl.BlockSpec((2, 256), lambda i, place: (0, i))],
            scratch_shapes=[pltpu.VMEM((256, 2048), BF16)],
        ),
        out_shape=[jax.ShapeDtypeStruct((32, 24, 128), F32)] * 2
        + [jax.ShapeDtypeStruct((2, WIDTH), F32)],
        compiler_params=pltpu.CompilerParams(
            vmem_limit_bytes=60 * MIB, dimension_semantics=("arbitrary",)
        ),
        cost_estimate=pl.CostEstimate(
            flops=2 * 2048 * WIDTH * 256, bytes_accessed=6 * MIB, transcendentals=0
        ),
        name="weight_grad",
    )(place, xhat, back, packed, w, w, w)


def pack_kernel(keep_ref, got_ref, sums_ref, out_ref):
    sums = jnp.concatenate(
        [sums_ref[c : c + 1, j * 128 : (j + 1) * 128] for c in range(2) for j in range(8)], axis=0
    )
    high = sums.astype(BF16).astype(F32)
    low = sums - high
    for t in range(32):
        piece = keep_ref[t] + got_ref[t]
        out_ref[t] = jnp.concatenate([piece[:16], high, low, piece[16:]], axis=0).astype(BF16)


def pack(keep, got, sums):
    return pl.pallas_call(
        pack_kernel,
        out_shape=jax.ShapeDtypeStruct((32, 56, 128), BF16),
        cost_estimate=pl.CostEstimate(flops=1 << 18, bytes_accessed=MIB, transcendentals=0),
        name="pack",
    )(keep, got, sums)


def collect_kernel(place_ref, pieces_ref, rows_ref, send_ref, keep_ref, other_ref):
    low = low_lanes((16, 128))
    half = low_lanes((8, 128))
    sums = [jnp.zeros((16, 128), F32)] * 2
    for pair in range(HEADS // 2):
        heads = []
        for head in (2 * pair, 2 * pair + 1):
            first = pieces_ref[2 * head].astype(F32)
            second = pieces_ref[2 * head + 1].astype(F32)
            heads.append(first + second)
            for z, part in enumerate((first, second)):
                sums[z] = sums[z] + (part[16:32] + part[32:48])
        dq, dk = pairs(low, heads[0][:16], heads[1][:16])
        dv = jnp.concatenate(pairs(half, heads[0][48:], heads[1][48:]), axis=0)
        for c, part in enumerate((dq, dk, dv)):
            lanes = slice(c * WIDTH + pair * 128, c * WIDTH + (pair + 1) * 128)
            rows_ref[:, lanes] = part
            send_ref[:, lanes] = part.astype(BF16)
    core = place_ref[0] == 0
    keep = jnp.where(core, sums[0], sums[1])
    other = jnp.where(core, sums[1], sums[0])
    for r in range(16):
        keep_ref[:, r * 128 : (r + 1) * 128] = keep[r : r + 1]
        other_ref[:, r * 128 : (r + 1) * 128] = other[r : r + 1]


def collect(place, pieces):
    return pl.pallas_call(
        collect_kernel,
        grid_spec=pltpu.PrefetchScalarGridSpec(
            num_scalar_prefetch=1,
            grid=(1,),
            in_specs=[pl.BlockSpec((32, 56, 128), lambda i, core: (0, 0, 0))],
            out_specs=[
                pl.BlockSpec((16, 3 * WIDTH), lambda i, core: (0, 0)),
                pl.BlockSpec((16, 3 * WIDTH), lambda i, core: (0, 0)),
                pl.BlockSpec((1, 2 * WIDTH), lambda i, core: (0, 0)),
                pl.BlockSpec((1, 2 * WIDTH), lambda i, core: (0, 0)),
            ],
        ),
        out_shape=[
            jax.ShapeDtypeStruct((16, 3 * WIDTH), F32),
            jax.ShapeDtypeStruct((16, 3 * WIDTH), BF16),
            jax.ShapeDtypeStruct((1, 2 * WIDTH), F32),
            jax.ShapeDtypeStruct((1, 2 * WIDTH), F32),
        ],
        cost_estimate=pl.CostEstimate(flops=1 << 20, bytes_accessed=MIB, transcendentals=0),
        name="collect",
    )(place, pieces)


def token_kernel(x_ref, mod_ref, back_ref, wq_ref, wk_ref, wv_ref, out_ref, acc):
    i = pl.program_id(0)
    low = low_lanes((TOK, 128))
    dq, dk, dv = [], [], []
    for p in range(2):
        a = back_ref[2 * p].astype(F32)
        b = back_ref[2 * p + 1].astype(F32)
        dq_pair, attended = pairs(low, a[:TOK], b[:TOK])
        dk_pair, dv_pair = pairs(low, a[TOK:], b[TOK:])
        lanes = pl.ds(pl.multiple_of(i * 256 + p * 128, 128), 128)
        out_ref[0, :, lanes] = attended.astype(BF16)
        dq.append(dq_pair.astype(BF16))
        dk.append(dk_pair.astype(BF16))
        dv.append(dv_pair.astype(BF16))
    part = (
        dot_t(jnp.concatenate(dq, axis=1), wq_ref[...])
        + dot_t(jnp.concatenate(dk, axis=1), wk_ref[...])
        + dot_t(jnp.concatenate(dv, axis=1), wv_ref[...])
    )

    @pl.when(i == 0)
    def _():
        acc[...] = part

    @pl.when(i > 0)
    def _():
        acc[...] += part

    @pl.when(i == pl.num_programs(0) - 1)
    def _():
        x = x_ref[...].astype(F32)
        inv = 1.0 / jnp.sqrt(jnp.mean(x * x, axis=1, keepdims=True) + 1e-06)
        xhat = x * inv
        dn = acc[...]
        gn = dn * (1.0 + mod_ref[0:1].astype(F32))
        out_ref[1] = (
            inv * (gn - xhat * jnp.mean(gn * xhat, axis=1, keepdims=True))
        ).astype(BF16)


def token_grad(packed, back, w):
    return pl.pallas_call(
        token_kernel,
        grid=(4,),
        in_specs=[
            pl.BlockSpec((TOK, WIDTH), lambda i: (0, 0)),
            pl.BlockSpec((16, WIDTH), lambda i: (16, 0)),
            pl.BlockSpec((4, 2 * TOK, 128), lambda i: (i, 0, 0)),
        ]
        + weight_specs(),
        out_specs=pl.BlockSpec((2, TOK, WIDTH), lambda i: (0, 0, 0)),
        out_shape=jax.ShapeDtypeStruct((2, TOK, WIDTH), BF16),
        scratch_shapes=[pltpu.VMEM((TOK, WIDTH), F32)],
        compiler_params=pltpu.CompilerParams(
            vmem_limit_bytes=60 * MIB, dimension_semantics=("arbitrary",)
        ),
        cost_estimate=pl.CostEstimate(
            flops=2 * TOK * WIDTH * 3 * WIDTH, bytes_accessed=8 * MIB, transcendentals=0
        ),
        name="token_grad",
    )(packed, packed, back, w, w, w)


def on_device(tokens, timestep, table, w_qkv, grad_out):
    core = lax.axis_index("dp") % 2
    head = lax.axis_index("tile") // 2
    place = jnp.stack([core, head % 2, head // 2]).astype(jnp.int32)
    row = lax.dynamic_slice(table, (timestep[0], 0), (1, 2 * WIDTH)).reshape(2, WIDTH)
    packed = swap(
        jnp.concatenate([tokens[0], grad_out[0], row, jnp.zeros((14, WIDTH), BF16)], axis=0)
    )
    copies, sent = project(packed, w_qkv)
    recv = plane_exchange(sent)
    copies, recv = lax.optimization_barrier((copies, recv))
    kvp = from_other_core(recv[:, TOK:])
    xhat = plane_exchange(copies).reshape(16 * TOK, WIDTH)
    back, own, other = attention(recv, kvp)
    back = combine(back, own, from_other_core(other))
    back_recv = plane_exchange(back)
    keep, send, sums = weight_grad(place, xhat, back, packed, w_qkv)
    packed_grads = pack(keep, from_other_core(send), sums)
    packed_grads, back_recv = lax.optimization_barrier((packed_grads, back_recv))
    pieces = lax.all_to_all(packed_grads, "tile", split_axis=0, concat_axis=0, tiled=True)
    out = token_grad(packed, back_recv, w_qkv)
    pieces, out = lax.optimization_barrier((pieces, out))
    out = swap(out)
    rows, rows_low, modulation, modulation_other = collect(place, pieces)
    modulation = modulation + from_other_core(modulation_other)
    for k in (2, 4, 6):
        rows = rows + lax.ppermute(rows_low, "dp", [(d, d ^ k) for d in range(8)]).astype(F32)
    rows, out = lax.optimization_barrier((rows, out))
    other_rows = from_other_core(rows)
    grad_wqkv = jnp.concatenate(
        [jnp.where(core == 0, rows, other_rows), jnp.where(core == 0, other_rows, rows)], axis=0
    )
    return (out[0][None], out[1][None], modulation, grad_wqkv)


def solution(mesh):
    placed = (P("dp", "tile", None), P("dp"), P(), P(), P("dp", "tile", None))
    return jax.shard_map(
        on_device,
        mesh=mesh,
        in_specs=placed,
        out_specs=(P("dp", "tile", None), P("dp", "tile", None), P("dp", None), P("tile", None)),
        check_vma=False,
    )
```

```python
import functools

import jax
import jax.numpy as jnp
from jax import lax
from jax.experimental import pallas as pl
from jax.experimental.pallas import tpu as pltpu
from jax.sharding import PartitionSpec as P

HEADS = 16
DEPTH = 64
WIDTH = 1024
TOK = 128
LOG2E = 1.4426950408889634
BF16 = jnp.bfloat16
F32 = jnp.float32
MIB = 1024 * 1024

SWAP = [
    ((zh * 2 + core) * 32 + yx * 2 + zl, (zh * 2 + zl) * 32 + yx * 2 + core)
    for zh in range(4)
    for core in range(2)
    for yx in range(16)
    for zl in range(2)
]
PLANE = [[yx * 2 + zl for yx in range(16)] for zl in range(2)]
OTHER_CORE = [(d, d ^ 1) for d in range(8)]


def swap(x):
    return lax.ppermute(x, ("dp", "tile"), SWAP)


def from_other_core(x):
    return lax.ppermute(x, "dp", OTHER_CORE)


def plane_exchange(x):
    return lax.all_to_all(
        x, "tile", split_axis=0, concat_axis=0, tiled=True, axis_index_groups=PLANE
    )


def dot(a, b):
    return jnp.dot(a, b, preferred_element_type=F32)


def dot_t(a, b):
    return lax.dot_general(a, b, (((1,), (1,)), ((), ())), preferred_element_type=F32)


def low_lanes(shape):
    return lax.broadcasted_iota(jnp.int32, shape, len(shape) - 1) < DEPTH


def pairs(low, a, b):
    axis = a.ndim - 1
    return jnp.where(low, a, pltpu.roll(b, DEPTH, axis)), jnp.where(
        low, pltpu.roll(a, DEPTH, axis), b
    )


def weight_copies(w_ref, w_vmem, sems):
    blocks = [pl.ds(i * 256, 256) for i in range(4)]
    return [
        pltpu.make_async_copy(w_ref.at[rows], w_vmem.at[rows], sems.at[i])
        for i, rows in enumerate(blocks)
    ]


def project_kernel(packed_ref, w_ref, copies_ref, out_ref, w_vmem, xhat_vmem, acc, w_sems, out_sems):
    loads = weight_copies(w_ref, w_vmem, w_sems)
    for load in loads:
        load.start()
    x = packed_ref[:TOK].astype(F32)
    inv = 1.0 / jnp.sqrt(jnp.mean(x * x, axis=1, keepdims=True) + 1e-06)
    xhat = x * inv
    xhat_vmem[...] = xhat.astype(BF16)
    stores = [
        pltpu.make_async_copy(xhat_vmem, copies_ref.at[t], out_sems.at[t]) for t in range(HEADS)
    ]
    for store in stores:
        store.start()
    mod = packed_ref[2 * TOK :].astype(F32)
    normed = (xhat * (1.0 + mod[0:1]) + mod[1:2]).astype(BF16)
    for i, load in enumerate(loads):
        load.wait()
        rows = slice(i * 256, (i + 1) * 256)
        part = dot(normed[:, rows], w_vmem[rows])
        if i == 0:
            acc[...] = part
        elif i < 3:
            acc[...] += part
    low = low_lanes((TOK, 128))
    for p in range(HEADS // 2):
        lanes = [slice(c * WIDTH + p * 128, c * WIDTH + (p + 1) * 128) for c in range(3)]
        q, k, v = [(acc[:, lane] + part[:, lane]).astype(BF16).astype(F32) for lane in lanes]
        g = packed_ref[TOK : 2 * TOK, lanes[0]].astype(F32)
        for rows, a, b in ((slice(0, TOK), q, g), (slice(TOK, 2 * TOK), k, v)):
            first, second = pairs(low, a, b)
            out_ref[2 * p, rows] = first.astype(BF16)
            out_ref[2 * p + 1, rows] = second.astype(BF16)
    for store in stores:
        store.wait()


def project(packed, w):
    vmem = pl.BlockSpec(memory_space=pltpu.VMEM)
    return pl.pallas_call(
        project_kernel,
        in_specs=[vmem, pl.BlockSpec(memory_space=pl.ANY)],
        out_specs=[pl.BlockSpec(memory_space=pl.ANY), vmem],
        out_shape=[
            jax.ShapeDtypeStruct((HEADS, TOK, WIDTH), BF16),
            jax.ShapeDtypeStruct((HEADS, 2 * TOK, 128), BF16),
        ],
        scratch_shapes=[
            pltpu.VMEM((WIDTH, 3 * WIDTH), BF16),
            pltpu.VMEM((TOK, WIDTH), BF16),
            pltpu.VMEM((TOK, 3 * WIDTH), F32),
            pltpu.SemaphoreType.DMA((4,)),
            pltpu.SemaphoreType.DMA((HEADS,)),
        ],
        compiler_params=pltpu.CompilerParams(vmem_limit_bytes=59 * MIB),
        cost_estimate=pl.CostEstimate(
            flops=2 * TOK * WIDTH * 3 * WIDTH, bytes_accessed=8 * MIB, transcendentals=0
        ),
        name="project",
    )(packed, w)


def attention_kernel(
    bq, kt, recv_ref, kvp_ref, back_ref, own_ref, other_ref, kv, kvt, acc, s_scr, dp_scr, pb_scr
):
    i = pl.program_id(0)
    nk = kv.shape[0]
    half = nk // 2
    tiles = [pl.ds(t * kt, kt) for t in range(nk // kt)]

    @pl.when(i == 0)
    def _():
        kv[:half] = recv_ref[:, 128:, :].reshape(half, 128)
        kv[half:] = kvp_ref[...].reshape(half, 128)
        acc[...] = jnp.zeros_like(acc)
        for t in tiles:
            kvt[:, t] = kv[t].T

    srcs = bq // 128
    qg = recv_ref[pl.ds(i * srcs, srcs), :128, :].reshape(bq, 128)
    low = low_lanes(qg.shape)
    zero = jnp.zeros_like(qg)
    q0 = jnp.where(low, qg * jnp.asarray(0.125, BF16), zero)
    g0 = jnp.where(low, zero, qg)
    q0t = q0.T
    g0t = g0.T
    top = jnp.full((8, bq), -jnp.inf, F32)
    for t in tiles:
        s = dot(kv[t], q0t)
        s_scr[t] = s
        top = jnp.maximum(top, jnp.max(s.reshape(kt // 8, 8, bq), axis=0))
    top = jnp.max(top, axis=0, keepdims=True)
    total = jnp.zeros((8, bq), F32)
    for t in tiles:
        e = jnp.exp2((s_scr[t] - top) * LOG2E)
        s_scr[t] = e
        total = total + jnp.sum(e.reshape(kt // 8, 8, bq), axis=0)
        dp_scr[t] = dot(kv[t], g0t)
    inv = 1.0 / jnp.sum(total, axis=0, keepdims=True)
    o_t = jnp.zeros((DEPTH, bq), F32)
    for t in tiles:
        pb = (s_scr[t] * inv).astype(BF16)
        pb_scr[t] = pb
        o_t = o_t + dot(kvt[DEPTH:, t], pb)
    delta = jnp.sum(o_t * g0t[DEPTH:].astype(F32), axis=0, keepdims=True)
    dq_t = jnp.zeros((DEPTH, bq), F32)
    for t in tiles:
        ds = ((s_scr[t] * inv) * (dp_scr[t] - delta)).astype(BF16)
        dq_t = dq_t + dot(kvt[:DEPTH, t], ds)
        acc[t] += dot(ds, q0) + dot(pb_scr[t], g0)
    dqo = jnp.concatenate([dq_t * 0.125, o_t], axis=0).T.astype(BF16)
    back_ref[:, :128] = dqo.reshape(srcs, 128, 128)

    @pl.when(i == pl.num_programs(0) - 1)
    def _():
        own_ref[...] = acc[:half].reshape(16, 128, 128)
        other_ref[...] = acc[half:].astype(BF16).reshape(16, 128, 128)


def attention(recv, kvp, bq=512, kt=256):
    nq, nk = 2048, 4096
    srcs = bq // 128
    whole = lambda i: (0, 0, 0)
    return pl.pallas_call(
        functools.partial(attention_kernel, bq, kt),
        grid=(nq // bq,),
        in_specs=[
            pl.BlockSpec((16, 256, 128), whole),
            pl.BlockSpec((16, 128, 128), whole),
        ],
        out_specs=[
            pl.BlockSpec((srcs, 256, 128), lambda i: (i, 0, 0)),
            pl.BlockSpec((16, 128, 128), whole),
            pl.BlockSpec((16, 128, 128), whole),
        ],
        out_shape=[
            jax.ShapeDtypeStruct((16, 256, 128), BF16),
            jax.ShapeDtypeStruct((16, 128, 128), F32),
            jax.ShapeDtypeStruct((16, 128, 128), BF16),
        ],
        scratch_shapes=[
            pltpu.VMEM((nk, 128), BF16),
            pltpu.VMEM((128, nk), BF16),
            pltpu.VMEM((nk, 128), F32),
            pltpu.VMEM((nk, bq), F32),
            pltpu.VMEM((nk, bq), F32),
            pltpu.VMEM((nk, bq), BF16),
        ],
        compiler_params=pltpu.CompilerParams(
            vmem_limit_bytes=48 * MIB, dimension_semantics=("arbitrary",)
        ),
        cost_estimate=pl.CostEstimate(
            flops=6 * 2 * nq * nk * 256, bytes_accessed=4 << 20, transcendentals=nq * nk
        ),
        name="attention",
    )(recv, kvp)


def combine_kernel(back_ref, own_ref, mine_ref, out_ref):
    out_ref[...] = (own_ref[...] + mine_ref[...].astype(F32)).astype(BF16)


def combine(back, own, mine):
    half = pl.BlockSpec((16, 128, 128), lambda i: (0, 0, 0))
    return pl.pallas_call(
        combine_kernel,
        grid=(1,),
        in_specs=[pl.BlockSpec(memory_space=pl.ANY), half, half],
        out_specs=pl.BlockSpec((16, 128, 128), lambda i: (0, 1, 0)),
        out_shape=jax.ShapeDtypeStruct((16, 256, 128), BF16),
        input_output_aliases={0: 0},
        compiler_params=pltpu.CompilerParams(vmem_limit_bytes=32 * MIB),
        cost_estimate=pl.CostEstimate(flops=1 << 18, bytes_accessed=2 * MIB, transcendentals=0),
        name="combine",
    )(back, own, mine)


def weight_kernel(
    place_ref, xhat_ref, back_ref, mod_ref, wq_ref, wk_ref, wv_ref, keep_ref, send_ref, sums_ref, back_t
):
    @pl.when(pl.program_id(0) == 0)
    def _():
        for s in range(16):
            tokens = slice(s * TOK, (s + 1) * TOK)
            back_t[:128, tokens] = back_ref[s, :TOK].T
            back_t[128:, tokens] = back_ref[s, TOK:].T

    lhs = back_t[...]
    grad_t = dot(lhs, xhat_ref[...])
    column = jnp.sum(lhs.astype(F32), axis=1, keepdims=True)
    odd = place_ref[1] == 1
    scale_sum = jnp.zeros((1, 256), F32)
    shift_sum = jnp.zeros((1, 256), F32)
    for w_ref, first in ((wq_ref, 0), (wk_ref, 128), (wv_ref, 192)):
        w_t = w_ref[...].astype(F32).T
        w_t = jnp.where(odd, w_t[DEPTH:], w_t[:DEPTH])
        rows = slice(first, first + DEPTH)
        scale_sum = scale_sum + jnp.sum(w_t * grad_t[rows], axis=0, keepdims=True)
        shift_sum = shift_sum + jnp.sum(w_t * column[rows], axis=0, keepdims=True)
    sums_ref[0:1] = scale_sum
    sums_ref[1:2] = shift_sum
    mod = mod_ref[...].astype(F32)
    grad = (grad_t * (1.0 + mod[0:1]) + column * mod[1:2]).T
    low = low_lanes((256, 128))
    dq_dk, dv = pairs(low, grad[:, :128], grad[:, 128:])
    dv = dv.reshape(8, 2, 2, 8, 128)
    low = low_lanes((8, 2, 8, 128))
    dv = jnp.where(low, pltpu.roll(dv[:, :, 0], DEPTH, 3), dv[:, :, 1])
    dq_dk = dq_dk.reshape(8, 2, 16, 128)

    def put(ref, half):
        ref[:, :16] = dq_dk[:, half]
        ref[:, 16:] = dv[:, half]

    @pl.when(place_ref[0] == 0)
    def _():
        put(keep_ref, 0)
        put(send_ref, 1)

    @pl.when(place_ref[0] == 1)
    def _():
        put(keep_ref, 1)
        put(send_ref, 0)


def weight_grad(place, xhat, back, packed, w):
    rows = pl.BlockSpec((8, 24, 128), lambda i, place: (i, 0, 0))
    return pl.pallas_call(
        weight_kernel,
        grid_spec=pltpu.PrefetchScalarGridSpec(
            num_scalar_prefetch=1,
            grid=(4,),
            in_specs=[
                pl.BlockSpec((2048, 256), lambda i, place: (0, i)),
                pl.BlockSpec((16, 256, 128), lambda i, place: (0, 0, 0)),
                pl.BlockSpec((16, 256), lambda i, place: (16, i)),
            ]
            + [pl.BlockSpec((256, 128), lambda i, place, c=c: (i, 8 * c + place[2])) for c in range(3)],
            out_specs=[rows, rows, pl.BlockSpec((2, 256), lambda i, place: (0, i))],
            scratch_shapes=[pltpu.VMEM((256, 2048), BF16)],
        ),
        out_shape=[jax.ShapeDtypeStruct((32, 24, 128), F32)] * 2
        + [jax.ShapeDtypeStruct((2, WIDTH), F32)],
        compiler_params=pltpu.CompilerParams(
            vmem_limit_bytes=60 * MIB, dimension_semantics=("arbitrary",)
        ),
        cost_estimate=pl.CostEstimate(
            flops=2 * 2048 * WIDTH * 256, bytes_accessed=6 * MIB, transcendentals=0
        ),
        name="weight_grad",
    )(place, xhat, back, packed, w, w, w)


def pack_kernel(keep_ref, got_ref, sums_ref, out_ref):
    sums = jnp.concatenate(
        [sums_ref[c : c + 1, j * 128 : (j + 1) * 128] for c in range(2) for j in range(8)], axis=0
    )
    high = sums.astype(BF16).astype(F32)
    low = sums - high
    for t in range(32):
        piece = keep_ref[t] + got_ref[t]
        out_ref[t] = jnp.concatenate([piece[:16], high, low, piece[16:]], axis=0).astype(BF16)


def pack(keep, got, sums):
    return pl.pallas_call(
        pack_kernel,
        out_shape=jax.ShapeDtypeStruct((32, 56, 128), BF16),
        compiler_params=pltpu.CompilerParams(vmem_limit_bytes=16 * MIB),
        cost_estimate=pl.CostEstimate(flops=1 << 18, bytes_accessed=MIB, transcendentals=0),
        name="pack",
    )(keep, got, sums)


def collect_kernel(place_ref, pieces_ref, rows_ref, send_ref, keep_ref, other_ref):
    low = low_lanes((16, 128))
    half = low_lanes((8, 128))
    sums = [jnp.zeros((16, 128), F32)] * 2
    for pair in range(HEADS // 2):
        heads = []
        for head in (2 * pair, 2 * pair + 1):
            first = pieces_ref[2 * head].astype(F32)
            second = pieces_ref[2 * head + 1].astype(F32)
            heads.append(first + second)
            for z, part in enumerate((first, second)):
                sums[z] = sums[z] + (part[16:32] + part[32:48])
        dq, dk = pairs(low, heads[0][:16], heads[1][:16])
        dv = jnp.concatenate(pairs(half, heads[0][48:], heads[1][48:]), axis=0)
        for c, part in enumerate((dq, dk, dv)):
            lanes = slice(c * WIDTH + pair * 128, c * WIDTH + (pair + 1) * 128)
            rows_ref[:, lanes] = part
            send_ref[:, lanes] = part.astype(BF16)
    core = place_ref[0] == 0
    keep = jnp.where(core, sums[0], sums[1])
    other = jnp.where(core, sums[1], sums[0])
    other_ref[...] = other
    for r in range(16):
        keep_ref[:, r * 128 : (r + 1) * 128] = keep[r : r + 1]


def collect(place, pieces):
    return pl.pallas_call(
        collect_kernel,
        grid_spec=pltpu.PrefetchScalarGridSpec(
            num_scalar_prefetch=1,
            grid=(1,),
            in_specs=[pl.BlockSpec((32, 56, 128), lambda i, core: (0, 0, 0))],
            out_specs=[
                pl.BlockSpec((16, 3 * WIDTH), lambda i, core: (0, 0)),
                pl.BlockSpec((16, 3 * WIDTH), lambda i, core: (0, 0)),
                pl.BlockSpec((1, 2 * WIDTH), lambda i, core: (0, 0)),
                pl.BlockSpec((16, 128), lambda i, core: (0, 0)),
            ],
        ),
        out_shape=[
            jax.ShapeDtypeStruct((16, 3 * WIDTH), F32),
            jax.ShapeDtypeStruct((16, 3 * WIDTH), BF16),
            jax.ShapeDtypeStruct((1, 2 * WIDTH), F32),
            jax.ShapeDtypeStruct((16, 128), F32),
        ],
        compiler_params=pltpu.CompilerParams(vmem_limit_bytes=16 * MIB),
        cost_estimate=pl.CostEstimate(flops=1 << 20, bytes_accessed=MIB, transcendentals=0),
        name="collect",
    )(place, pieces)


def weight_column_copies(w_ref, w_vmem, sems):
    groups = []
    for i in range(4):
        group = []
        for c in range(3):
            lanes = slice(c * WIDTH + i * 256, c * WIDTH + (i + 1) * 256)
            group.append(
                pltpu.make_async_copy(w_ref.at[:, lanes], w_vmem.at[:, lanes], sems.at[3 * i + c])
            )
        groups.append(group)
    return groups


def token_kernel(packed_ref, back_ref, w_ref, out_ref, w_vmem, w_sems):
    loads = weight_column_copies(w_ref, w_vmem, w_sems)
    for group in loads:
        for load in group:
            load.start()
    low = low_lanes((TOK, 128))
    dn = jnp.zeros((TOK, WIDTH), F32)
    for i, group in enumerate(loads):
        parts = [[], [], []]
        for p in range(2):
            a = back_ref[4 * i + 2 * p].astype(F32)
            b = back_ref[4 * i + 2 * p + 1].astype(F32)
            dq_pair, attended = pairs(low, a[:TOK], b[:TOK])
            dk_pair, dv_pair = pairs(low, a[TOK:], b[TOK:])
            out_ref[0, :, i * 256 + p * 128 : i * 256 + (p + 1) * 128] = attended.astype(BF16)
            for part, pair in zip(parts, (dq_pair, dk_pair, dv_pair)):
                part.append(pair.astype(BF16))
        for c, load in enumerate(group):
            load.wait()
            lanes = slice(c * WIDTH + i * 256, c * WIDTH + (i + 1) * 256)
            dn = dn + dot_t(jnp.concatenate(parts[c], axis=1), w_vmem[:, lanes])
    x = packed_ref[:TOK].astype(F32)
    inv = 1.0 / jnp.sqrt(jnp.mean(x * x, axis=1, keepdims=True) + 1e-06)
    xhat = x * inv
    gn = dn * (1.0 + packed_ref[2 * TOK :].astype(F32)[0:1])
    out_ref[1] = (inv * (gn - xhat * jnp.mean(gn * xhat, axis=1, keepdims=True))).astype(BF16)


def token_grad(packed, back, w):
    vmem = pl.BlockSpec(memory_space=pltpu.VMEM)
    return pl.pallas_call(
        token_kernel,
        in_specs=[vmem, vmem, pl.BlockSpec(memory_space=pl.ANY)],
        out_specs=vmem,
        out_shape=jax.ShapeDtypeStruct((2, TOK, WIDTH), BF16),
        scratch_shapes=[
            pltpu.VMEM((WIDTH, 3 * WIDTH), BF16),
            pltpu.SemaphoreType.DMA((12,)),
        ],
        compiler_params=pltpu.CompilerParams(vmem_limit_bytes=59 * MIB),
        cost_estimate=pl.CostEstimate(
            flops=2 * TOK * WIDTH * 3 * WIDTH, bytes_accessed=8 * MIB, transcendentals=0
        ),
        name="token_grad",
    )(packed, back, w)


def on_device(tokens, timestep, table, w_qkv, grad_out):
    core = lax.axis_index("dp") % 2
    head = lax.axis_index("tile") // 2
    place = jnp.stack([core, head % 2, head // 2]).astype(jnp.int32)
    row = lax.dynamic_slice(table, (timestep[0], 0), (1, 2 * WIDTH)).reshape(2, WIDTH)
    packed = swap(
        jnp.concatenate([tokens[0], grad_out[0], row, jnp.zeros((14, WIDTH), BF16)], axis=0)
    )
    copies, sent = project(packed, w_qkv)
    recv = plane_exchange(sent)
    copies, recv = lax.optimization_barrier((copies, recv))
    kvp = from_other_core(recv[:, TOK:])
    xhat = plane_exchange(copies).reshape(16 * TOK, WIDTH)
    back, own, other = attention(recv, kvp)
    back = combine(back, own, from_other_core(other))
    back_recv = plane_exchange(back)
    keep, send, sums = weight_grad(place, xhat, back, packed, w_qkv)
    packed_grads = pack(keep, from_other_core(send), sums)
    packed_grads, back_recv = lax.optimization_barrier((packed_grads, back_recv))
    pieces = lax.all_to_all(packed_grads, "tile", split_axis=0, concat_axis=0, tiled=True)
    out = token_grad(packed, back_recv, w_qkv)
    pieces, out = lax.optimization_barrier((pieces, out))
    out = swap(out)
    rows, rows_low, modulation, modulation_other = collect(place, pieces)
    for k in (2, 4, 6):
        rows = rows + lax.ppermute(rows_low, "dp", [(d, d ^ k) for d in range(8)]).astype(F32)
    other_rows = from_other_core(jnp.concatenate([rows, modulation_other], axis=1))
    modulation = modulation + other_rows[:, 3 * WIDTH :].reshape(1, 2 * WIDTH)
    other_rows = other_rows[:, : 3 * WIDTH]
    other_rows, out = lax.optimization_barrier((other_rows, out))
    grad_wqkv = jnp.concatenate(
        [jnp.where(core == 0, rows, other_rows), jnp.where(core == 0, other_rows, rows)], axis=0
    )
    return (out[0][None], out[1][None], modulation, grad_wqkv)


def solution(mesh):
    placed = (P("dp", "tile", None), P("dp"), P(), P(), P("dp", "tile", None))
    return jax.shard_map(
        on_device,
        mesh=mesh,
        in_specs=placed,
        out_specs=(P("dp", "tile", None), P("dp", "tile", None), P("dp", None), P("tile", None)),
        check_vma=False,
    )
```

```python
import functools

import jax
import jax.numpy as jnp
from jax import lax
from jax.experimental import pallas as pl
from jax.experimental.pallas import tpu as pltpu
from jax.sharding import PartitionSpec as P

HEADS = 16
DEPTH = 64
WIDTH = 1024
TOK = 128
LOG2E = 1.4426950408889634
BF16 = jnp.bfloat16
F32 = jnp.float32
MIB = 1024 * 1024

SWAP = [
    ((zh * 2 + core) * 32 + yx * 2 + zl, (zh * 2 + zl) * 32 + yx * 2 + core)
    for zh in range(4)
    for core in range(2)
    for yx in range(16)
    for zl in range(2)
]
PLANE = [[yx * 2 + zl for yx in range(16)] for zl in range(2)]
OTHER_CORE = [(d, d ^ 1) for d in range(8)]


def swap(x):
    return lax.ppermute(x, ("dp", "tile"), SWAP)


def from_other_core(x):
    return lax.ppermute(x, "dp", OTHER_CORE)


def plane_exchange(x):
    return lax.all_to_all(
        x, "tile", split_axis=0, concat_axis=0, tiled=True, axis_index_groups=PLANE
    )


def dot(a, b):
    return jnp.dot(a, b, preferred_element_type=F32)


def dot_t(a, b):
    return lax.dot_general(a, b, (((1,), (1,)), ((), ())), preferred_element_type=F32)


def low_lanes(shape):
    return lax.broadcasted_iota(jnp.int32, shape, len(shape) - 1) < DEPTH


def pairs(low, a, b):
    axis = a.ndim - 1
    return jnp.where(low, a, pltpu.roll(b, DEPTH, axis)), jnp.where(
        low, pltpu.roll(a, DEPTH, axis), b
    )


def weight_copies(w_ref, w_vmem, sems):
    blocks = [pl.ds(i * 256, 256) for i in range(4)]
    return [
        pltpu.make_async_copy(w_ref.at[rows], w_vmem.at[rows], sems.at[i])
        for i, rows in enumerate(blocks)
    ]


def project_kernel(packed_ref, w_ref, copies_ref, out_ref, w_vmem, xhat_vmem, acc, w_sems, out_sems):
    loads = weight_copies(w_ref, w_vmem, w_sems)
    for load in loads:
        load.start()
    x = packed_ref[:TOK].astype(F32)
    inv = 1.0 / jnp.sqrt(jnp.mean(x * x, axis=1, keepdims=True) + 1e-06)
    xhat = x * inv
    xhat_vmem[...] = xhat.astype(BF16)
    stores = [
        pltpu.make_async_copy(xhat_vmem, copies_ref.at[t], out_sems.at[t]) for t in range(HEADS)
    ]
    for store in stores:
        store.start()
    mod = packed_ref[TOK:].astype(F32)
    normed = (xhat * (1.0 + mod[0:1]) + mod[1:2]).astype(BF16)
    for i, load in enumerate(loads):
        load.wait()
        rows = slice(i * 256, (i + 1) * 256)
        part = dot(normed[:, rows], w_vmem[rows])
        if i == 0:
            acc[...] = part
        elif i < 3:
            acc[...] += part
    low = low_lanes((TOK, 128))
    for p in range(HEADS // 2):
        lanes = [slice(c * WIDTH + p * 128, c * WIDTH + (p + 1) * 128) for c in range(3)]
        q, k, v = [(acc[:, lane] + part[:, lane]).astype(BF16).astype(F32) for lane in lanes]
        out_ref[2 * p, :TOK] = q.astype(BF16)
        out_ref[2 * p + 1, :TOK] = pltpu.roll(q, DEPTH, 1).astype(BF16)
        first, second = pairs(low, k, v)
        out_ref[2 * p, TOK:] = first.astype(BF16)
        out_ref[2 * p + 1, TOK:] = second.astype(BF16)
    for store in stores:
        store.wait()


def project(packed, w):
    vmem = pl.BlockSpec(memory_space=pltpu.VMEM)
    return pl.pallas_call(
        project_kernel,
        in_specs=[vmem, pl.BlockSpec(memory_space=pl.ANY)],
        out_specs=[pl.BlockSpec(memory_space=pl.ANY), vmem],
        out_shape=[
            jax.ShapeDtypeStruct((HEADS, TOK, WIDTH), BF16),
            jax.ShapeDtypeStruct((HEADS, 2 * TOK, 128), BF16),
        ],
        scratch_shapes=[
            pltpu.VMEM((WIDTH, 3 * WIDTH), BF16),
            pltpu.VMEM((TOK, WIDTH), BF16),
            pltpu.VMEM((TOK, 3 * WIDTH), F32),
            pltpu.SemaphoreType.DMA((4,)),
            pltpu.SemaphoreType.DMA((HEADS,)),
        ],
        compiler_params=pltpu.CompilerParams(vmem_limit_bytes=59 * MIB),
        cost_estimate=pl.CostEstimate(
            flops=2 * TOK * WIDTH * 3 * WIDTH, bytes_accessed=8 * MIB, transcendentals=0
        ),
        name="project",
    )(packed, w)


def cotangent_kernel(queries_ref, g_ref, out_ref):
    low = low_lanes((TOK, 128))
    for p in range(HEADS // 2):
        g = g_ref[:, p * 128 : (p + 1) * 128].astype(F32)
        for head, part in ((2 * p, pltpu.roll(g, DEPTH, 1)), (2 * p + 1, g)):
            out_ref[head] = jnp.where(low, queries_ref[head].astype(F32), part).astype(BF16)


def add_cotangents(sent, g):
    queries = pl.BlockSpec((HEADS, TOK, 128), lambda i: (0, 0, 0))
    return pl.pallas_call(
        cotangent_kernel,
        grid=(1,),
        in_specs=[queries, pl.BlockSpec((TOK, WIDTH), lambda i: (0, 0))],
        out_specs=queries,
        out_shape=jax.ShapeDtypeStruct((HEADS, 2 * TOK, 128), BF16),
        input_output_aliases={0: 0},
        compiler_params=pltpu.CompilerParams(vmem_limit_bytes=32 * MIB),
        cost_estimate=pl.CostEstimate(flops=1 << 18, bytes_accessed=2 * MIB, transcendentals=0),
        name="add_cotangents",
    )(sent, g)


def attention_kernel(
    bq, kt, recv_ref, kvp_ref, back_ref, own_ref, other_ref, kv, kvt, acc, s_scr, dp_scr, pb_scr
):
    i = pl.program_id(0)
    nk = kv.shape[0]
    half = nk // 2
    tiles = [pl.ds(t * kt, kt) for t in range(nk // kt)]

    @pl.when(i == 0)
    def _():
        kv[:half] = recv_ref[:, 128:, :].reshape(half, 128)
        kv[half:] = kvp_ref[...].reshape(half, 128)
        acc[...] = jnp.zeros_like(acc)
        for t in tiles:
            kvt[:, t] = kv[t].T

    srcs = bq // 128
    qg = recv_ref[pl.ds(i * srcs, srcs), :128, :].reshape(bq, 128)
    low = low_lanes(qg.shape)
    zero = jnp.zeros_like(qg)
    q0 = jnp.where(low, qg * jnp.asarray(0.125, BF16), zero)
    g0 = jnp.where(low, zero, qg)
    q0t = q0.T
    g0t = g0.T
    top = jnp.full((8, bq), -jnp.inf, F32)
    for t in tiles:
        s = dot(kv[t], q0t)
        s_scr[t] = s
        top = jnp.maximum(top, jnp.max(s.reshape(kt // 8, 8, bq), axis=0))
    top = jnp.max(top, axis=0, keepdims=True)
    total = jnp.zeros((8, bq), F32)
    for t in tiles:
        e = jnp.exp2((s_scr[t] - top) * LOG2E)
        s_scr[t] = e
        total = total + jnp.sum(e.reshape(kt // 8, 8, bq), axis=0)
        dp_scr[t] = dot(kv[t], g0t)
    inv = 1.0 / jnp.sum(total, axis=0, keepdims=True)
    o_t = jnp.zeros((DEPTH, bq), F32)
    for t in tiles:
        pb = (s_scr[t] * inv).astype(BF16)
        pb_scr[t] = pb
        o_t = o_t + dot(kvt[DEPTH:, t], pb)
    delta = jnp.sum(o_t * g0t[DEPTH:].astype(F32), axis=0, keepdims=True)
    dq_t = jnp.zeros((DEPTH, bq), F32)
    for t in tiles:
        ds = ((s_scr[t] * inv) * (dp_scr[t] - delta)).astype(BF16)
        dq_t = dq_t + dot(kvt[:DEPTH, t], ds)
        acc[t] += dot(ds, q0) + dot(pb_scr[t], g0)
    dqo = jnp.concatenate([dq_t * 0.125, o_t], axis=0).T.astype(BF16)
    back_ref[:, :128] = dqo.reshape(srcs, 128, 128)

    @pl.when(i == pl.num_programs(0) - 1)
    def _():
        own_ref[...] = acc[:half].reshape(16, 128, 128)
        other_ref[...] = acc[half:].astype(BF16).reshape(16, 128, 128)


def attention(recv, kvp, bq=512, kt=256):
    nq, nk = 2048, 4096
    srcs = bq // 128
    whole = lambda i: (0, 0, 0)
    return pl.pallas_call(
        functools.partial(attention_kernel, bq, kt),
        grid=(nq // bq,),
        in_specs=[
            pl.BlockSpec((16, 256, 128), whole),
            pl.BlockSpec((16, 128, 128), whole),
        ],
        out_specs=[
            pl.BlockSpec((srcs, 256, 128), lambda i: (i, 0, 0)),
            pl.BlockSpec((16, 128, 128), whole),
            pl.BlockSpec((16, 128, 128), whole),
        ],
        out_shape=[
            jax.ShapeDtypeStruct((16, 256, 128), BF16),
            jax.ShapeDtypeStruct((16, 128, 128), F32),
            jax.ShapeDtypeStruct((16, 128, 128), BF16),
        ],
        scratch_shapes=[
            pltpu.VMEM((nk, 128), BF16),
            pltpu.VMEM((128, nk), BF16),
            pltpu.VMEM((nk, 128), F32),
            pltpu.VMEM((nk, bq), F32),
            pltpu.VMEM((nk, bq), F32),
            pltpu.VMEM((nk, bq), BF16),
        ],
        compiler_params=pltpu.CompilerParams(
            vmem_limit_bytes=48 * MIB, dimension_semantics=("arbitrary",)
        ),
        cost_estimate=pl.CostEstimate(
            flops=6 * 2 * nq * nk * 256, bytes_accessed=4 << 20, transcendentals=nq * nk
        ),
        name="attention",
    )(recv, kvp)


def combine_kernel(back_ref, own_ref, mine_ref, out_ref):
    out_ref[...] = (own_ref[...] + mine_ref[...].astype(F32)).astype(BF16)


def combine(back, own, mine):
    half = pl.BlockSpec((16, 128, 128), lambda i: (0, 0, 0))
    return pl.pallas_call(
        combine_kernel,
        grid=(1,),
        in_specs=[pl.BlockSpec(memory_space=pl.ANY), half, half],
        out_specs=pl.BlockSpec((16, 128, 128), lambda i: (0, 1, 0)),
        out_shape=jax.ShapeDtypeStruct((16, 256, 128), BF16),
        input_output_aliases={0: 0},
        compiler_params=pltpu.CompilerParams(vmem_limit_bytes=32 * MIB),
        cost_estimate=pl.CostEstimate(flops=1 << 18, bytes_accessed=2 * MIB, transcendentals=0),
        name="combine",
    )(back, own, mine)


def weight_kernel(
    place_ref, xhat_ref, back_ref, mod_ref, wq_ref, wk_ref, wv_ref, keep_ref, send_ref, sums_ref, back_t
):
    @pl.when(pl.program_id(0) == 0)
    def _():
        for s in range(16):
            tokens = slice(s * TOK, (s + 1) * TOK)
            back_t[:128, tokens] = back_ref[s, :TOK].T
            back_t[128:, tokens] = back_ref[s, TOK:].T

    lhs = back_t[...]
    grad_t = dot(lhs, xhat_ref[...])
    column = jnp.sum(lhs.astype(F32), axis=1, keepdims=True)
    odd = place_ref[1] == 1
    scale_sum = jnp.zeros((1, 256), F32)
    shift_sum = jnp.zeros((1, 256), F32)
    for w_ref, first in ((wq_ref, 0), (wk_ref, 128), (wv_ref, 192)):
        w_t = w_ref[...].astype(F32).T
        w_t = jnp.where(odd, w_t[DEPTH:], w_t[:DEPTH])
        rows = slice(first, first + DEPTH)
        scale_sum = scale_sum + jnp.sum(w_t * grad_t[rows], axis=0, keepdims=True)
        shift_sum = shift_sum + jnp.sum(w_t * column[rows], axis=0, keepdims=True)
    sums_ref[0:1] = scale_sum
    sums_ref[1:2] = shift_sum
    mod = mod_ref[...].astype(F32)
    grad = (grad_t * (1.0 + mod[0:1]) + column * mod[1:2]).T
    low = low_lanes((256, 128))
    dq_dk, dv = pairs(low, grad[:, :128], grad[:, 128:])
    dv = dv.reshape(8, 2, 2, 8, 128)
    low = low_lanes((8, 2, 8, 128))
    dv = jnp.where(low, pltpu.roll(dv[:, :, 0], DEPTH, 3), dv[:, :, 1])
    dq_dk = dq_dk.reshape(8, 2, 16, 128)

    def put(ref, half):
        ref[:, :16] = dq_dk[:, half]
        ref[:, 16:] = dv[:, half]

    @pl.when(place_ref[0] == 0)
    def _():
        put(keep_ref, 0)
        put(send_ref, 1)

    @pl.when(place_ref[0] == 1)
    def _():
        put(keep_ref, 1)
        put(send_ref, 0)


def weight_grad(place, xhat, back, packed, w):
    rows = pl.BlockSpec((8, 24, 128), lambda i, place: (i, 0, 0))
    return pl.pallas_call(
        weight_kernel,
        grid_spec=pltpu.PrefetchScalarGridSpec(
            num_scalar_prefetch=1,
            grid=(4,),
            in_specs=[
                pl.BlockSpec((2048, 256), lambda i, place: (0, i)),
                pl.BlockSpec((16, 256, 128), lambda i, place: (0, 0, 0)),
                pl.BlockSpec((16, 256), lambda i, place: (8, i)),
            ]
            + [pl.BlockSpec((256, 128), lambda i, place, c=c: (i, 8 * c + place[2])) for c in range(3)],
            out_specs=[rows, rows, pl.BlockSpec((2, 256), lambda i, place: (0, i))],
            scratch_shapes=[pltpu.VMEM((256, 2048), BF16)],
        ),
        out_shape=[jax.ShapeDtypeStruct((32, 24, 128), F32)] * 2
        + [jax.ShapeDtypeStruct((2, WIDTH), F32)],
        compiler_params=pltpu.CompilerParams(
            vmem_limit_bytes=60 * MIB, dimension_semantics=("arbitrary",)
        ),
        cost_estimate=pl.CostEstimate(
            flops=2 * 2048 * WIDTH * 256, bytes_accessed=6 * MIB, transcendentals=0
        ),
        name="weight_grad",
    )(place, xhat, back, packed, w, w, w)


def pack_kernel(keep_ref, got_ref, sums_ref, out_ref):
    sums = jnp.concatenate(
        [sums_ref[c : c + 1, j * 128 : (j + 1) * 128] for c in range(2) for j in range(8)], axis=0
    )
    high = sums.astype(BF16).astype(F32)
    low = sums - high
    for t in range(32):
        piece = keep_ref[t] + got_ref[t]
        out_ref[t] = jnp.concatenate([piece[:16], high, low, piece[16:]], axis=0).astype(BF16)


def pack(keep, got, sums):
    return pl.pallas_call(
        pack_kernel,
        out_shape=jax.ShapeDtypeStruct((32, 56, 128), BF16),
        compiler_params=pltpu.CompilerParams(vmem_limit_bytes=16 * MIB),
        cost_estimate=pl.CostEstimate(flops=1 << 18, bytes_accessed=MIB, transcendentals=0),
        name="pack",
    )(keep, got, sums)


def collect_kernel(place_ref, pieces_ref, rows_ref, send_ref, keep_ref, other_ref):
    low = low_lanes((16, 128))
    half = low_lanes((8, 128))
    sums = [jnp.zeros((16, 128), F32)] * 2
    for pair in range(HEADS // 2):
        heads = []
        for head in (2 * pair, 2 * pair + 1):
            first = pieces_ref[2 * head].astype(F32)
            second = pieces_ref[2 * head + 1].astype(F32)
            heads.append(first + second)
            for z, part in enumerate((first, second)):
                sums[z] = sums[z] + (part[16:32] + part[32:48])
        dq, dk = pairs(low, heads[0][:16], heads[1][:16])
        dv = jnp.concatenate(pairs(half, heads[0][48:], heads[1][48:]), axis=0)
        for c, part in enumerate((dq, dk, dv)):
            lanes = slice(c * WIDTH + pair * 128, c * WIDTH + (pair + 1) * 128)
            rows_ref[:, lanes] = part
            send_ref[:, lanes] = part.astype(BF16)
    core = place_ref[0] == 0
    keep = jnp.where(core, sums[0], sums[1])
    other = jnp.where(core, sums[1], sums[0])
    other_ref[...] = other
    for r in range(16):
        keep_ref[:, r * 128 : (r + 1) * 128] = keep[r : r + 1]


def collect(place, pieces):
    return pl.pallas_call(
        collect_kernel,
        grid_spec=pltpu.PrefetchScalarGridSpec(
            num_scalar_prefetch=1,
            grid=(1,),
            in_specs=[pl.BlockSpec((32, 56, 128), lambda i, core: (0, 0, 0))],
            out_specs=[
                pl.BlockSpec((16, 3 * WIDTH), lambda i, core: (0, 0)),
                pl.BlockSpec((16, 3 * WIDTH), lambda i, core: (0, 0)),
                pl.BlockSpec((1, 2 * WIDTH), lambda i, core: (0, 0)),
                pl.BlockSpec((16, 128), lambda i, core: (0, 0)),
            ],
        ),
        out_shape=[
            jax.ShapeDtypeStruct((16, 3 * WIDTH), F32),
            jax.ShapeDtypeStruct((16, 3 * WIDTH), BF16),
            jax.ShapeDtypeStruct((1, 2 * WIDTH), F32),
            jax.ShapeDtypeStruct((16, 128), F32),
        ],
        compiler_params=pltpu.CompilerParams(vmem_limit_bytes=16 * MIB),
        cost_estimate=pl.CostEstimate(flops=1 << 20, bytes_accessed=MIB, transcendentals=0),
        name="collect",
    )(place, pieces)


def weight_column_copies(w_ref, w_vmem, sems):
    groups = []
    for i in range(4):
        group = []
        for c in range(3):
            lanes = slice(c * WIDTH + i * 256, c * WIDTH + (i + 1) * 256)
            group.append(
                pltpu.make_async_copy(w_ref.at[:, lanes], w_vmem.at[:, lanes], sems.at[3 * i + c])
            )
        groups.append(group)
    return groups


def token_kernel(packed_ref, back_ref, w_ref, out_ref, w_vmem, w_sems):
    loads = weight_column_copies(w_ref, w_vmem, w_sems)
    for group in loads:
        for load in group:
            load.start()
    low = low_lanes((TOK, 128))
    dn = jnp.zeros((TOK, WIDTH), F32)
    for i, group in enumerate(loads):
        parts = [[], [], []]
        for p in range(2):
            a = back_ref[4 * i + 2 * p].astype(F32)
            b = back_ref[4 * i + 2 * p + 1].astype(F32)
            dq_pair, attended = pairs(low, a[:TOK], b[:TOK])
            dk_pair, dv_pair = pairs(low, a[TOK:], b[TOK:])
            out_ref[0, :, i * 256 + p * 128 : i * 256 + (p + 1) * 128] = attended.astype(BF16)
            for part, pair in zip(parts, (dq_pair, dk_pair, dv_pair)):
                part.append(pair.astype(BF16))
        for c, load in enumerate(group):
            load.wait()
            lanes = slice(c * WIDTH + i * 256, c * WIDTH + (i + 1) * 256)
            dn = dn + dot_t(jnp.concatenate(parts[c], axis=1), w_vmem[:, lanes])
    x = packed_ref[:TOK].astype(F32)
    inv = 1.0 / jnp.sqrt(jnp.mean(x * x, axis=1, keepdims=True) + 1e-06)
    xhat = x * inv
    gn = dn * (1.0 + packed_ref[TOK:].astype(F32)[0:1])
    out_ref[1] = (inv * (gn - xhat * jnp.mean(gn * xhat, axis=1, keepdims=True))).astype(BF16)


def token_grad(packed, back, w):
    vmem = pl.BlockSpec(memory_space=pltpu.VMEM)
    return pl.pallas_call(
        token_kernel,
        in_specs=[vmem, vmem, pl.BlockSpec(memory_space=pl.ANY)],
        out_specs=vmem,
        out_shape=jax.ShapeDtypeStruct((2, TOK, WIDTH), BF16),
        scratch_shapes=[
            pltpu.VMEM((WIDTH, 3 * WIDTH), BF16),
            pltpu.SemaphoreType.DMA((12,)),
        ],
        compiler_params=pltpu.CompilerParams(vmem_limit_bytes=59 * MIB),
        cost_estimate=pl.CostEstimate(
            flops=2 * TOK * WIDTH * 3 * WIDTH, bytes_accessed=8 * MIB, transcendentals=0
        ),
        name="token_grad",
    )(packed, back, w)


def on_device(tokens, timestep, table, w_qkv, grad_out):
    core = lax.axis_index("dp") % 2
    head = lax.axis_index("tile") // 2
    place = jnp.stack([core, head % 2, head // 2]).astype(jnp.int32)
    row = lax.dynamic_slice(table, (timestep[0], 0), (1, 2 * WIDTH)).reshape(2, WIDTH)
    packed = swap(jnp.concatenate([tokens[0], row, jnp.zeros((14, WIDTH), BF16)], axis=0))
    g = swap(grad_out[0])
    copies, sent = project(packed, w_qkv)
    recv = plane_exchange(add_cotangents(sent, g))
    copies, recv = lax.optimization_barrier((copies, recv))
    kvp = from_other_core(recv[:, TOK:])
    xhat = plane_exchange(copies).reshape(16 * TOK, WIDTH)
    back, own, other = attention(recv, kvp)
    back = combine(back, own, from_other_core(other))
    back_recv = plane_exchange(back)
    keep, send, sums = weight_grad(place, xhat, back, packed, w_qkv)
    packed_grads = pack(keep, from_other_core(send), sums)
    packed_grads, back_recv = lax.optimization_barrier((packed_grads, back_recv))
    pieces = lax.all_to_all(packed_grads, "tile", split_axis=0, concat_axis=0, tiled=True)
    out = token_grad(packed, back_recv, w_qkv)
    pieces, out = lax.optimization_barrier((pieces, out))
    out = swap(out)
    rows, rows_low, modulation, modulation_other = collect(place, pieces)
    for k in (2, 4, 6):
        rows = rows + lax.ppermute(rows_low, "dp", [(d, d ^ k) for d in range(8)]).astype(F32)
    other_rows = from_other_core(jnp.concatenate([rows, modulation_other], axis=1))
    modulation = modulation + other_rows[:, 3 * WIDTH :].reshape(1, 2 * WIDTH)
    other_rows = other_rows[:, : 3 * WIDTH]
    other_rows, out = lax.optimization_barrier((other_rows, out))
    grad_wqkv = jnp.concatenate(
        [jnp.where(core == 0, rows, other_rows), jnp.where(core == 0, other_rows, rows)], axis=0
    )
    return (out[0][None], out[1][None], modulation, grad_wqkv)


def solution(mesh):
    placed = (P("dp", "tile", None), P("dp"), P(), P(), P("dp", "tile", None))
    return jax.shard_map(
        on_device,
        mesh=mesh,
        in_specs=placed,
        out_specs=(P("dp", "tile", None), P("dp", "tile", None), P("dp", None), P("tile", None)),
        check_vma=False,
    )
```

```python
import functools

import jax
import jax.numpy as jnp
from jax import lax
from jax.experimental import pallas as pl
from jax.experimental.pallas import tpu as pltpu
from jax.sharding import PartitionSpec as P

HEADS = 16
DEPTH = 64
WIDTH = 1024
TOK = 128
LOG2E = 1.4426950408889634
BF16 = jnp.bfloat16
F32 = jnp.float32
MIB = 1024 * 1024

SWAP = [
    ((zh * 2 + core) * 32 + yx * 2 + zl, (zh * 2 + zl) * 32 + yx * 2 + core)
    for zh in range(4)
    for core in range(2)
    for yx in range(16)
    for zl in range(2)
]
PLANE = [[yx * 2 + zl for yx in range(16)] for zl in range(2)]
OTHER_CORE = [(d, d ^ 1) for d in range(8)]


def swap(x):
    return lax.ppermute(x, ("dp", "tile"), SWAP)


def from_other_core(x):
    return lax.ppermute(x, "dp", OTHER_CORE)


def plane_exchange(x):
    return lax.all_to_all(
        x, "tile", split_axis=0, concat_axis=0, tiled=True, axis_index_groups=PLANE
    )


def dot(a, b):
    return jnp.dot(a, b, preferred_element_type=F32)


def dot_t(a, b):
    return lax.dot_general(a, b, (((1,), (1,)), ((), ())), preferred_element_type=F32)


def low_lanes(shape):
    return lax.broadcasted_iota(jnp.int32, shape, len(shape) - 1) < DEPTH


def pairs(low, a, b):
    axis = a.ndim - 1
    return jnp.where(low, a, pltpu.roll(b, DEPTH, axis)), jnp.where(
        low, pltpu.roll(a, DEPTH, axis), b
    )


def weight_copies(w_ref, w_vmem, sems):
    blocks = [pl.ds(i * 256, 256) for i in range(4)]
    return [
        pltpu.make_async_copy(w_ref.at[rows], w_vmem.at[rows], sems.at[i])
        for i, rows in enumerate(blocks)
    ]


def project_kernel(packed_ref, g_ref, w_ref, copies_ref, out_ref, w_vmem, xhat_vmem, acc, w_sems, out_sems):
    loads = weight_copies(w_ref, w_vmem, w_sems)
    for load in loads:
        load.start()
    x = packed_ref[:TOK].astype(F32)
    inv = 1.0 / jnp.sqrt(jnp.mean(x * x, axis=1, keepdims=True) + 1e-06)
    xhat = x * inv
    xhat_vmem[...] = xhat.astype(BF16)
    stores = [
        pltpu.make_async_copy(xhat_vmem, copies_ref.at[t], out_sems.at[t]) for t in range(HEADS)
    ]
    for store in stores:
        store.start()
    mod = packed_ref[TOK:].astype(F32)
    normed = (xhat * (1.0 + mod[0:1]) + mod[1:2]).astype(BF16)
    for i, load in enumerate(loads):
        load.wait()
        rows = slice(i * 256, (i + 1) * 256)
        part = dot(normed[:, rows], w_vmem[rows])
        if i == 0:
            acc[...] = part
        elif i < 3:
            acc[...] += part
    low = low_lanes((TOK, 128))
    for p in range(HEADS // 2):
        lanes = [slice(c * WIDTH + p * 128, c * WIDTH + (p + 1) * 128) for c in range(3)]
        q, k, v = [(acc[:, lane] + part[:, lane]).astype(BF16).astype(F32) for lane in lanes]
        g = g_ref[:, lanes[0]].astype(F32)
        for rows, a, b in ((slice(0, TOK), q, g), (slice(TOK, 2 * TOK), k, v)):
            first, second = pairs(low, a, b)
            out_ref[2 * p, rows] = first.astype(BF16)
            out_ref[2 * p + 1, rows] = second.astype(BF16)
    for store in stores:
        store.wait()


def project(packed, g, w):
    vmem = pl.BlockSpec(memory_space=pltpu.VMEM)
    return pl.pallas_call(
        project_kernel,
        in_specs=[vmem, vmem, pl.BlockSpec(memory_space=pl.ANY)],
        out_specs=[pl.BlockSpec(memory_space=pl.ANY), vmem],
        out_shape=[
            jax.ShapeDtypeStruct((HEADS, TOK, WIDTH), BF16),
            jax.ShapeDtypeStruct((HEADS, 2 * TOK, 128), BF16),
        ],
        scratch_shapes=[
            pltpu.VMEM((WIDTH, 3 * WIDTH), BF16),
            pltpu.VMEM((TOK, WIDTH), BF16),
            pltpu.VMEM((TOK, 3 * WIDTH), F32),
            pltpu.SemaphoreType.DMA((4,)),
            pltpu.SemaphoreType.DMA((HEADS,)),
        ],
        compiler_params=pltpu.CompilerParams(vmem_limit_bytes=59 * MIB),
        cost_estimate=pl.CostEstimate(
            flops=2 * TOK * WIDTH * 3 * WIDTH, bytes_accessed=8 * MIB, transcendentals=0
        ),
        name="project",
    )(packed, g, w)


def attention_kernel(
    bq, kt, recv_ref, kvp_ref, back_ref, own_ref, other_ref, kv, kvt, acc, s_scr, dp_scr, pb_scr
):
    i = pl.program_id(0)
    nk = kv.shape[0]
    half = nk // 2
    tiles = [pl.ds(t * kt, kt) for t in range(nk // kt)]

    @pl.when(i == 0)
    def _():
        kv[:half] = recv_ref[:, 128:, :].reshape(half, 128)
        kv[half:] = kvp_ref[...].reshape(half, 128)
        acc[...] = jnp.zeros_like(acc)
        for t in tiles:
            kvt[:, t] = kv[t].T

    srcs = bq // 128
    qg = recv_ref[pl.ds(i * srcs, srcs), :128, :].reshape(bq, 128)
    low = low_lanes(qg.shape)
    zero = jnp.zeros_like(qg)
    q0 = jnp.where(low, qg * jnp.asarray(0.125, BF16), zero)
    g0 = jnp.where(low, zero, qg)
    q0t = q0.T
    g0t = g0.T
    top = jnp.full((8, bq), -jnp.inf, F32)
    for t in tiles:
        s = dot(kv[t], q0t)
        s_scr[t] = s
        top = jnp.maximum(top, jnp.max(s.reshape(kt // 8, 8, bq), axis=0))
    top = jnp.max(top, axis=0, keepdims=True)
    total = jnp.zeros((8, bq), F32)
    for t in tiles:
        e = jnp.exp2((s_scr[t] - top) * LOG2E)
        s_scr[t] = e
        total = total + jnp.sum(e.reshape(kt // 8, 8, bq), axis=0)
        dp_scr[t] = dot(kv[t], g0t)
    inv = 1.0 / jnp.sum(total, axis=0, keepdims=True)
    o_t = jnp.zeros((DEPTH, bq), F32)
    for t in tiles:
        pb = (s_scr[t] * inv).astype(BF16)
        pb_scr[t] = pb
        o_t = o_t + dot(kvt[DEPTH:, t], pb)
    delta = jnp.sum(o_t * g0t[DEPTH:].astype(F32), axis=0, keepdims=True)
    dq_t = jnp.zeros((DEPTH, bq), F32)
    for t in tiles:
        ds = ((s_scr[t] * inv) * (dp_scr[t] - delta)).astype(BF16)
        dq_t = dq_t + dot(kvt[:DEPTH, t], ds)
        acc[t] += dot(ds, q0) + dot(pb_scr[t], g0)
    dqo = jnp.concatenate([dq_t * 0.125, o_t], axis=0).T.astype(BF16)
    back_ref[:, :128] = dqo.reshape(srcs, 128, 128)

    @pl.when(i == pl.num_programs(0) - 1)
    def _():
        own_ref[...] = acc[:half].reshape(16, 128, 128)
        other_ref[...] = acc[half:].astype(BF16).reshape(16, 128, 128)


def attention(recv, kvp, bq=512, kt=256):
    nq, nk = 2048, 4096
    srcs = bq // 128
    whole = lambda i: (0, 0, 0)
    return pl.pallas_call(
        functools.partial(attention_kernel, bq, kt),
        grid=(nq // bq,),
        in_specs=[
            pl.BlockSpec((16, 256, 128), whole),
            pl.BlockSpec((16, 128, 128), whole),
        ],
        out_specs=[
            pl.BlockSpec((srcs, 256, 128), lambda i: (i, 0, 0)),
            pl.BlockSpec((16, 128, 128), whole),
            pl.BlockSpec((16, 128, 128), whole),
        ],
        out_shape=[
            jax.ShapeDtypeStruct((16, 256, 128), BF16),
            jax.ShapeDtypeStruct((16, 128, 128), F32),
            jax.ShapeDtypeStruct((16, 128, 128), BF16),
        ],
        scratch_shapes=[
            pltpu.VMEM((nk, 128), BF16),
            pltpu.VMEM((128, nk), BF16),
            pltpu.VMEM((nk, 128), F32),
            pltpu.VMEM((nk, bq), F32),
            pltpu.VMEM((nk, bq), F32),
            pltpu.VMEM((nk, bq), BF16),
        ],
        compiler_params=pltpu.CompilerParams(
            vmem_limit_bytes=48 * MIB, dimension_semantics=("arbitrary",)
        ),
        cost_estimate=pl.CostEstimate(
            flops=6 * 2 * nq * nk * 256, bytes_accessed=4 << 20, transcendentals=nq * nk
        ),
        name="attention",
    )(recv, kvp)


def combine_kernel(back_ref, own_ref, mine_ref, out_ref):
    out_ref[...] = (own_ref[...] + mine_ref[...].astype(F32)).astype(BF16)


def combine(back, own, mine):
    half = pl.BlockSpec((16, 128, 128), lambda i: (0, 0, 0))
    return pl.pallas_call(
        combine_kernel,
        grid=(1,),
        in_specs=[pl.BlockSpec(memory_space=pl.ANY), half, half],
        out_specs=pl.BlockSpec((16, 128, 128), lambda i: (0, 1, 0)),
        out_shape=jax.ShapeDtypeStruct((16, 256, 128), BF16),
        input_output_aliases={0: 0},
        compiler_params=pltpu.CompilerParams(vmem_limit_bytes=32 * MIB),
        cost_estimate=pl.CostEstimate(flops=1 << 18, bytes_accessed=2 * MIB, transcendentals=0),
        name="combine",
    )(back, own, mine)


def weight_kernel(
    place_ref, xhat_ref, back_ref, mod_ref, wq_ref, wk_ref, wv_ref, keep_ref, send_ref, sums_ref, back_t
):
    @pl.when(pl.program_id(0) == 0)
    def _():
        for s in range(16):
            tokens = slice(s * TOK, (s + 1) * TOK)
            back_t[:128, tokens] = back_ref[s, :TOK].T
            back_t[128:, tokens] = back_ref[s, TOK:].T

    lhs = back_t[...]
    grad_t = dot(lhs, xhat_ref[...])
    column = jnp.sum(lhs.astype(F32), axis=1, keepdims=True)
    odd = place_ref[1] == 1
    scale_sum = jnp.zeros((1, 256), F32)
    shift_sum = jnp.zeros((1, 256), F32)
    for w_ref, first in ((wq_ref, 0), (wk_ref, 128), (wv_ref, 192)):
        w_t = w_ref[...].astype(F32).T
        w_t = jnp.where(odd, w_t[DEPTH:], w_t[:DEPTH])
        rows = slice(first, first + DEPTH)
        scale_sum = scale_sum + jnp.sum(w_t * grad_t[rows], axis=0, keepdims=True)
        shift_sum = shift_sum + jnp.sum(w_t * column[rows], axis=0, keepdims=True)
    sums_ref[0:1] = scale_sum
    sums_ref[1:2] = shift_sum
    mod = mod_ref[...].astype(F32)
    grad = (grad_t * (1.0 + mod[0:1]) + column * mod[1:2]).T
    low = low_lanes((256, 128))
    dq_dk, dv = pairs(low, grad[:, :128], grad[:, 128:])
    dv = dv.reshape(8, 2, 2, 8, 128)
    low = low_lanes((8, 2, 8, 128))
    dv = jnp.where(low, pltpu.roll(dv[:, :, 0], DEPTH, 3), dv[:, :, 1])
    dq_dk = dq_dk.reshape(8, 2, 16, 128)

    def put(ref, half):
        ref[:, :16] = dq_dk[:, half]
        ref[:, 16:] = dv[:, half]

    @pl.when(place_ref[0] == 0)
    def _():
        put(keep_ref, 0)
        put(send_ref, 1)

    @pl.when(place_ref[0] == 1)
    def _():
        put(keep_ref, 1)
        put(send_ref, 0)


def weight_grad(place, xhat, back, packed, w):
    rows = pl.BlockSpec((8, 24, 128), lambda i, place: (i, 0, 0))
    return pl.pallas_call(
        weight_kernel,
        grid_spec=pltpu.PrefetchScalarGridSpec(
            num_scalar_prefetch=1,
            grid=(4,),
            in_specs=[
                pl.BlockSpec((2048, 256), lambda i, place: (0, i)),
                pl.BlockSpec((16, 256, 128), lambda i, place: (0, 0, 0)),
                pl.BlockSpec((16, 256), lambda i, place: (8, i)),
            ]
            + [pl.BlockSpec((256, 128), lambda i, place, c=c: (i, 8 * c + place[2])) for c in range(3)],
            out_specs=[rows, rows, pl.BlockSpec((2, 256), lambda i, place: (0, i))],
            scratch_shapes=[pltpu.VMEM((256, 2048), BF16)],
        ),
        out_shape=[jax.ShapeDtypeStruct((32, 24, 128), F32)] * 2
        + [jax.ShapeDtypeStruct((2, WIDTH), F32)],
        compiler_params=pltpu.CompilerParams(
            vmem_limit_bytes=60 * MIB, dimension_semantics=("arbitrary",)
        ),
        cost_estimate=pl.CostEstimate(
            flops=2 * 2048 * WIDTH * 256, bytes_accessed=6 * MIB, transcendentals=0
        ),
        name="weight_grad",
    )(place, xhat, back, packed, w, w, w)


def pack_kernel(keep_ref, got_ref, sums_ref, out_ref):
    sums = jnp.concatenate(
        [sums_ref[c : c + 1, j * 128 : (j + 1) * 128] for c in range(2) for j in range(8)], axis=0
    )
    high = sums.astype(BF16).astype(F32)
    low = sums - high
    for t in range(32):
        piece = keep_ref[t] + got_ref[t]
        out_ref[t] = jnp.concatenate([piece[:16], high, low, piece[16:]], axis=0).astype(BF16)


def pack(keep, got, sums):
    return pl.pallas_call(
        pack_kernel,
        out_shape=jax.ShapeDtypeStruct((32, 56, 128), BF16),
        compiler_params=pltpu.CompilerParams(vmem_limit_bytes=16 * MIB),
        cost_estimate=pl.CostEstimate(flops=1 << 18, bytes_accessed=MIB, transcendentals=0),
        name="pack",
    )(keep, got, sums)


def collect_kernel(place_ref, pieces_ref, rows_ref, send_ref, keep_ref, other_ref):
    low = low_lanes((16, 128))
    half = low_lanes((8, 128))
    sums = [jnp.zeros((16, 128), F32)] * 2
    for pair in range(HEADS // 2):
        heads = []
        for head in (2 * pair, 2 * pair + 1):
            first = pieces_ref[2 * head].astype(F32)
            second = pieces_ref[2 * head + 1].astype(F32)
            heads.append(first + second)
            for z, part in enumerate((first, second)):
                sums[z] = sums[z] + (part[16:32] + part[32:48])
        dq, dk = pairs(low, heads[0][:16], heads[1][:16])
        dv = jnp.concatenate(pairs(half, heads[0][48:], heads[1][48:]), axis=0)
        for c, part in enumerate((dq, dk, dv)):
            lanes = slice(c * WIDTH + pair * 128, c * WIDTH + (pair + 1) * 128)
            rows_ref[:, lanes] = part
            send_ref[:, lanes] = part.astype(BF16)
    core = place_ref[0] == 0
    keep = jnp.where(core, sums[0], sums[1])
    other = jnp.where(core, sums[1], sums[0])
    other_ref[...] = other
    for r in range(16):
        keep_ref[:, r * 128 : (r + 1) * 128] = keep[r : r + 1]


def collect(place, pieces):
    return pl.pallas_call(
        collect_kernel,
        grid_spec=pltpu.PrefetchScalarGridSpec(
            num_scalar_prefetch=1,
            grid=(1,),
            in_specs=[pl.BlockSpec((32, 56, 128), lambda i, core: (0, 0, 0))],
            out_specs=[
                pl.BlockSpec((16, 3 * WIDTH), lambda i, core: (0, 0)),
                pl.BlockSpec((16, 3 * WIDTH), lambda i, core: (0, 0)),
                pl.BlockSpec((1, 2 * WIDTH), lambda i, core: (0, 0)),
                pl.BlockSpec((16, 128), lambda i, core: (0, 0)),
            ],
        ),
        out_shape=[
            jax.ShapeDtypeStruct((16, 3 * WIDTH), F32),
            jax.ShapeDtypeStruct((16, 3 * WIDTH), BF16),
            jax.ShapeDtypeStruct((1, 2 * WIDTH), F32),
            jax.ShapeDtypeStruct((16, 128), F32),
        ],
        compiler_params=pltpu.CompilerParams(vmem_limit_bytes=16 * MIB),
        cost_estimate=pl.CostEstimate(flops=1 << 20, bytes_accessed=MIB, transcendentals=0),
        name="collect",
    )(place, pieces)


def weight_column_copies(w_ref, w_vmem, sems):
    groups = []
    for i in range(4):
        group = []
        for c in range(3):
            lanes = slice(c * WIDTH + i * 256, c * WIDTH + (i + 1) * 256)
            group.append(
                pltpu.make_async_copy(w_ref.at[:, lanes], w_vmem.at[:, lanes], sems.at[3 * i + c])
            )
        groups.append(group)
    return groups


def token_kernel(packed_ref, back_ref, w_ref, out_ref, w_vmem, w_sems):
    loads = weight_column_copies(w_ref, w_vmem, w_sems)
    for group in loads:
        for load in group:
            load.start()
    low = low_lanes((TOK, 128))
    dn = jnp.zeros((TOK, WIDTH), F32)
    for i, group in enumerate(loads):
        parts = [[], [], []]
        for p in range(2):
            a = back_ref[4 * i + 2 * p].astype(F32)
            b = back_ref[4 * i + 2 * p + 1].astype(F32)
            dq_pair, attended = pairs(low, a[:TOK], b[:TOK])
            dk_pair, dv_pair = pairs(low, a[TOK:], b[TOK:])
            out_ref[0, :, i * 256 + p * 128 : i * 256 + (p + 1) * 128] = attended.astype(BF16)
            for part, pair in zip(parts, (dq_pair, dk_pair, dv_pair)):
                part.append(pair.astype(BF16))
        for c, load in enumerate(group):
            load.wait()
            lanes = slice(c * WIDTH + i * 256, c * WIDTH + (i + 1) * 256)
            dn = dn + dot_t(jnp.concatenate(parts[c], axis=1), w_vmem[:, lanes])
    x = packed_ref[:TOK].astype(F32)
    inv = 1.0 / jnp.sqrt(jnp.mean(x * x, axis=1, keepdims=True) + 1e-06)
    xhat = x * inv
    gn = dn * (1.0 + packed_ref[TOK:].astype(F32)[0:1])
    out_ref[1] = (inv * (gn - xhat * jnp.mean(gn * xhat, axis=1, keepdims=True))).astype(BF16)


def token_grad(packed, back, w):
    vmem = pl.BlockSpec(memory_space=pltpu.VMEM)
    return pl.pallas_call(
        token_kernel,
        in_specs=[vmem, vmem, pl.BlockSpec(memory_space=pl.ANY)],
        out_specs=vmem,
        out_shape=jax.ShapeDtypeStruct((2, TOK, WIDTH), BF16),
        scratch_shapes=[
            pltpu.VMEM((WIDTH, 3 * WIDTH), BF16),
            pltpu.SemaphoreType.DMA((12,)),
        ],
        compiler_params=pltpu.CompilerParams(vmem_limit_bytes=59 * MIB),
        cost_estimate=pl.CostEstimate(
            flops=2 * TOK * WIDTH * 3 * WIDTH, bytes_accessed=8 * MIB, transcendentals=0
        ),
        name="token_grad",
    )(packed, back, w)


def on_device(tokens, timestep, table, w_qkv, grad_out):
    core = lax.axis_index("dp") % 2
    head = lax.axis_index("tile") // 2
    place = jnp.stack([core, head % 2, head // 2]).astype(jnp.int32)
    row = lax.dynamic_slice(table, (timestep[0], 0), (1, 2 * WIDTH)).reshape(2, WIDTH)
    packed = swap(jnp.concatenate([tokens[0], row, jnp.zeros((14, WIDTH), BF16)], axis=0))
    g = swap(grad_out[0])
    copies, sent = project(packed, g, w_qkv)
    recv = plane_exchange(sent)
    copies, recv = lax.optimization_barrier((copies, recv))
    kvp = from_other_core(recv[:, TOK:])
    xhat = plane_exchange(copies).reshape(16 * TOK, WIDTH)
    back, own, other = attention(recv, kvp)
    back = combine(back, own, from_other_core(other))
    back_recv = plane_exchange(back)
    keep, send, sums = weight_grad(place, xhat, back, packed, w_qkv)
    packed_grads = pack(keep, from_other_core(send), sums)
    packed_grads, back_recv = lax.optimization_barrier((packed_grads, back_recv))
    pieces = lax.all_to_all(packed_grads, "tile", split_axis=0, concat_axis=0, tiled=True)
    out = token_grad(packed, back_recv, w_qkv)
    pieces, out = lax.optimization_barrier((pieces, out))
    out = swap(out)
    rows, rows_low, modulation, modulation_other = collect(place, pieces)
    for k in (2, 4, 6):
        rows = rows + lax.ppermute(rows_low, "dp", [(d, d ^ k) for d in range(8)]).astype(F32)
    other_rows = from_other_core(jnp.concatenate([rows, modulation_other], axis=1))
    modulation = modulation + other_rows[:, 3 * WIDTH :].reshape(1, 2 * WIDTH)
    other_rows = other_rows[:, : 3 * WIDTH]
    other_rows, out = lax.optimization_barrier((other_rows, out))
    grad_wqkv = jnp.concatenate(
        [jnp.where(core == 0, rows, other_rows), jnp.where(core == 0, other_rows, rows)], axis=0
    )
    return (out[0][None], out[1][None], modulation, grad_wqkv)


def solution(mesh):
    placed = (P("dp", "tile", None), P("dp"), P(), P(), P("dp", "tile", None))
    return jax.shard_map(
        on_device,
        mesh=mesh,
        in_specs=placed,
        out_specs=(P("dp", "tile", None), P("dp", "tile", None), P("dp", None), P("tile", None)),
        check_vma=False,
    )
```
